32 devices in a mesh: seq: 16 (over z, x, core), branch: 2 (over y).
Axes of the slice: x: 2, y: 2, z: 4, core: 2. Of those that a mesh axis runs over, the one named last changes fastest.
Arguments:
- queries: bfloat16 [2, 896, 2560], P('branch', 'seq'), may hold values from -100 to 100
- keys_values: bfloat16 [2, 896, 2560], P(None, 'seq', 'branch'), may hold values from -10 to 10
- residual_in: bfloat16 [2, 896, 2560], P('branch', 'seq'), may hold values from -90 to 90
- cross_gain: bfloat16 [2560], replicated, may hold values from 0.099609375 to 1.8984375
- text_kv: bfloat16 [2, 2, 512, 2560], replicated, may hold values from -90 to 90
- prompt_ids: int32 [2, 512], replicated, may hold values from 0 to 256383
- word_align: int32 [512], replicated, may hold values from 0 to 511, as said below
Outputs:
- attended: bfloat16 [2, 896, 2560], P('branch', 'seq')
- result: bfloat16 [2, 896, 2560], P('branch', 'seq')
The draws below stay inside these ranges and needn't reach their ends.
Inputs may be any that keep to these rules, and one draw needn't show every extreme that they name: `word_align`: a permutation of the 512 source positions.
All inputs are finite; a program needn't handle non-finite values.
Results may differ from the reference program's by a relative error of at most 0.019.
Values may be sent and summed in bfloat16 or wider, within the bound.
A program may use at most 128 MiB of HBM per device.

```python
import math
import jax
import jax.numpy as jnp
from jax import lax

H = 20
HD = 128
TXT = 512
VOCAB = 256384
W = 2560
TOKENS = 896


def attention_draw(key):
    parts = jax.random.split(jax.random.fold_in(key, 11), 3)
    width = H * HD
    key_rows = jnp.clip(jax.random.normal(parts[0], (TOKENS, width), jnp.float32), -5.0, 5.0)
    value_rows = jnp.clip(2.0 * jax.random.normal(parts[1], (TOKENS, width), jnp.float32), -10.0, 10.0)
    query_rows = jnp.clip(2.0 * jax.random.normal(parts[2], (2, TOKENS, width), jnp.float32), -8.0, 8.0)
    return (query_rows, jnp.stack([key_rows, value_rows]))


def draw_queries(key, part):
    return attention_draw(key)[0].astype(jnp.bfloat16)


def draw_keys_values(key, part):
    return attention_draw(key)[1].astype(jnp.bfloat16)


def text_draw(key):
    parts = jax.random.split(jax.random.fold_in(key, 23), 4)
    width = H * HD
    residual = jnp.clip(0.3 * jax.random.normal(parts[1], (2, TOKENS, width), jnp.float32), -2.0, 2.0)
    text_keys = jnp.clip(2.0 * jax.random.normal(parts[2], (2, TXT, width), jnp.float32), -10.0, 10.0)
    text_values = jnp.clip(4.0 * jax.random.normal(parts[3], (2, TXT, width), jnp.float32), -24.0, 24.0)
    return (residual, jnp.stack([text_keys, text_values]))


def draw_residual_in(key, part):
    return text_draw(key)[0].astype(jnp.bfloat16)


def draw_text_kv(key, part):
    return text_draw(key)[1].astype(jnp.bfloat16)


def prompt_draw(key):
    parts = jax.random.split(jax.random.fold_in(key, 37), 4)
    source_ids = jax.random.randint(parts[0], (TXT,), 0, VOCAB, dtype=jnp.int32)
    source_ids = source_ids.at[0].set(VOCAB - 1).at[1].set(0)
    position = jnp.arange(TXT, dtype=jnp.int32)
    order_score = 8 * position + jax.random.randint(parts[1], (TXT,), 0, 24, dtype=jnp.int32)
    order_score = order_score * TXT + position
    word_order = jnp.argsort(order_score).astype(jnp.int32)
    fresh_ids = jax.random.randint(parts[2], (TXT,), 0, VOCAB, dtype=jnp.int32)
    replaced = jax.random.randint(parts[3], (TXT,), 0, 4, dtype=jnp.int32) == 0
    edit_ids = jnp.where(replaced, fresh_ids, source_ids[word_order])
    return (jnp.stack([source_ids, edit_ids]).astype(jnp.int32), word_order)


def draw_prompt_ids(key, part):
    return prompt_draw(key)[0]


def draw_word_align(key, part):
    return prompt_draw(key)[1]


def setup_inputs(seed: int = 0) -> dict:
    seeds = jax.random.split(jax.random.key(seed), 8)
    queries = draw_queries(jax.random.fold_in(seeds[7], 71), 0)
    keys_values = draw_keys_values(jax.random.fold_in(seeds[7], 71), 0)
    residual_in = draw_residual_in(jax.random.fold_in(seeds[7], 71), 0)
    cross_gain = jnp.clip(1.0 + 0.18 * jax.random.normal(seeds[3], (W,), jnp.float32), 0.099609375, 1.8984375).astype(jnp.bfloat16)
    text_kv = draw_text_kv(jax.random.fold_in(seeds[7], 71), 0)
    prompt_ids = draw_prompt_ids(jax.random.fold_in(seeds[7], 71), 0)
    word_align = draw_word_align(jax.random.fold_in(seeds[7], 71), 0)
    return {"queries": queries, "keys_values": keys_values, "residual_in": residual_in, "cross_gain": cross_gain, "text_kv": text_kv, "prompt_ids": prompt_ids, "word_align": word_align}


def softmax_parts(scores):
    row_peak = lax.optimization_barrier(jnp.max(scores, axis=-1, keepdims=True))
    weights = jnp.exp(scores - row_peak)
    return (weights, lax.optimization_barrier(jnp.sum(weights, axis=-1, keepdims=True)))

def alignment(prompt_ids, word_align):
    word_pairs = jnp.arange(TXT, dtype=jnp.int32)[:, None] == word_align[None, :]
    aligned_ids = lax.optimization_barrier(jnp.sum(jnp.where(word_pairs, prompt_ids[0][:, None], 0), axis=0))
    same_word = prompt_ids[1] == aligned_ids
    selection = jnp.where(word_pairs & same_word[None, :], 1.0, 0.0).astype(jnp.float32)
    keep_own = jnp.where(same_word, 0.0, 1.0).astype(jnp.float32)
    return (selection, keep_own)

def self_attention(queries, keys_values):
    score_scale = 1.0 / math.sqrt(HD)
    query_heads = queries.reshape(2 * TOKENS, H, HD).transpose(1, 0, 2)
    key_heads = keys_values[0].reshape(TOKENS, H, HD).transpose(1, 0, 2)
    value_heads = keys_values[1].reshape(TOKENS, H, HD).transpose(1, 0, 2)

    def one_head(operands):
        query_rows, key_rows, value_rows = operands
        scores = jnp.dot(query_rows, key_rows.T, preferred_element_type=jnp.float32) * score_scale
        weights, weight_sum = softmax_parts(scores)
        summed = jnp.dot(weights.astype(jnp.bfloat16), value_rows, preferred_element_type=jnp.float32)
        return summed / weight_sum
    output = lax.map(one_head, (query_heads, key_heads, value_heads))
    return output.transpose(1, 0, 2).reshape(2, TOKENS, H * HD).astype(jnp.bfloat16)

def text_maps(cross_query, text_keys):
    query_heads = cross_query.astype(jnp.float32).reshape(TOKENS, H, HD)
    key_heads = text_keys.astype(jnp.float32).reshape(TXT, H, HD)
    scores = jnp.einsum('qhd,thd->hqt', query_heads, key_heads) * (1.0 / math.sqrt(HD))
    weights, weight_sum = softmax_parts(scores)
    return weights / weight_sum

def reference(queries, keys_values, residual_in, cross_gain, text_kv, prompt_ids, word_align):
    attended = self_attention(queries, keys_values)
    middle = residual_in.astype(jnp.float32) + attended.astype(jnp.float32)
    cross_query = (middle * lax.rsqrt(lax.optimization_barrier(jnp.mean(middle * middle, axis=-1, keepdims=True)) + 1e-06) * cross_gain.astype(jnp.float32)).astype(jnp.bfloat16)
    selection, keep_own = alignment(prompt_ids, word_align)
    source_maps = text_maps(cross_query[0], text_kv[0, 0]).astype(jnp.bfloat16)
    edit_maps = text_maps(cross_query[1], text_kv[0, 1])
    picked = jnp.einsum('hqs,sj->hqj', source_maps.astype(jnp.float32), selection)
    injected = (picked + edit_maps * keep_own).astype(jnp.bfloat16)
    outputs = []
    for branch, map_set in ((0, source_maps), (1, injected)):
        value_rows = text_kv[1, branch].astype(jnp.float32).reshape(TXT, H, HD)
        outputs.append(jnp.einsum('hqt,thd->qhd', map_set.astype(jnp.float32), value_rows).reshape(TOKENS, H * HD))
    result = (middle + jnp.stack(outputs)).astype(jnp.bfloat16)
    return (attended, result)
```

```python
import functools
import math

import jax
import jax.numpy as jnp
from jax import lax
from jax.experimental import pallas as pl
from jax.experimental.pallas import tpu as pltpu
from jax.sharding import PartitionSpec as P

HD = 128
PAIR = 2
MESH = pl.DeviceIdType.MESH


def rows_by_rows(left, right):
    return lax.dot_general(
        left, right, (((1,), (1,)), ((), ())), preferred_element_type=jnp.float32
    )


def kernel(
    n,
    q_ref,
    kv_ref,
    res_ref,
    gain_ref,
    text_ref,
    ids_ref,
    align_ref,
    att_ref,
    out_ref,
    q_all,
    r_all,
    kv_all,
    text,
    moved,
    place,
    probs,
    totals,
    att,
    mid,
    squares,
    out,
    text_sem,
    own_sem,
    own_out_sem,
    recv_sem,
    send_z,
    send_x,
    send_c,
    y_send,
    y_recv,
    back_send,
    back_recv,
):
    rows = q_ref.shape[0]
    half = kv_ref.shape[2]
    heads = half // HD
    pairs = heads // PAIR
    wide = PAIR * HD
    text_len = text_ref.shape[2]
    tall = n // 4
    scale = 1.0 / math.sqrt(HD)
    me = lax.axis_index("seq")
    branch = lax.axis_index("branch")
    other = 1 - branch
    core = me % 2
    side = (me // 2) % 2
    level = me // 4
    mine = pl.multiple_of(branch * half, HD)
    theirs = pl.multiple_of(other * half, HD)

    def index(lev, sid, cor):
        return lev * 4 + sid * 2 + cor

    x_peer = index(level, 1 - side, core)
    c_peer = index(level, side, 1 - core)

    def text_copy(i):
        return pltpu.make_async_copy(
            text_ref.at[i // 2, i % 2, :, pl.ds(mine, half)], text.at[i], text_sem.at[i]
        )

    for i in range(4):
        text_copy(i).start()

    def own_copy(i):
        if i == 0:
            return pltpu.make_async_copy(
                q_ref.at[:, pl.ds(mine, half)], q_all.at[branch], own_sem.at[0]
            )
        if i == 1:
            return pltpu.make_async_copy(
                res_ref.at[:, pl.ds(mine, half)], r_all.at[branch], own_sem.at[1]
            )
        return pltpu.make_async_copy(kv_ref.at[i - 2], kv_all.at[me, i - 2], own_sem.at[i])

    for i in range(4):
        own_copy(i).start()

    barrier = pltpu.get_barrier_semaphore()

    def greet(seq, bra):
        pl.semaphore_signal(barrier, inc=1, device_id=(seq, bra), device_id_type=MESH)

    def z_peer(step):
        return index((level + step) % tall, side, core)

    @pl.loop(1, tall)
    def _(step):
        greet(z_peer(step), branch)

    greet(x_peer, branch)
    greet(c_peer, branch)
    greet(me, other)
    pl.semaphore_wait(barrier, tall + 2)

    def kv_copy(source, origin, which, peer, sem):
        return pltpu.make_async_remote_copy(
            src_ref=source,
            dst_ref=kv_all.at[origin, which],
            send_sem=sem,
            recv_sem=recv_sem.at[origin, which],
            device_id=(peer, branch),
            device_id_type=MESH,
        )

    def to_z(step, which):
        return kv_copy(kv_ref.at[which], me, which, z_peer(step), send_z.at[step, which])

    def to_x(lev, which, own):
        origin = index(lev, side, core)
        source = kv_ref.at[which] if own else kv_all.at[origin, which]
        return kv_copy(source, origin, which, x_peer, send_x.at[lev, which])

    def to_c(lev, sid, which, own):
        origin = index(lev, sid, core)
        source = kv_ref.at[which] if own else kv_all.at[origin, which]
        return kv_copy(source, origin, which, c_peer, send_c.at[lev * 2 + sid, which])

    def arrived(origin, which):
        pltpu.make_async_remote_copy(
            src_ref=kv_all.at[origin, which],
            dst_ref=kv_all.at[origin, which],
            send_sem=send_x.at[0, which],
            recv_sem=recv_sem.at[origin, which],
            device_id=(x_peer, branch),
            device_id_type=MESH,
        ).wait_recv()

    def y_copy(i):
        source, target = ((q_ref, q_all), (res_ref, r_all))[i]
        return pltpu.make_async_remote_copy(
            src_ref=source.at[:, pl.ds(theirs, half)],
            dst_ref=target.at[branch],
            send_sem=y_send.at[i],
            recv_sem=y_recv.at[i],
            device_id=(me, other),
            device_id_type=MESH,
        )

    def send_own(which):
        to_x(level, which, True).start()

        @pl.loop(1, tall)
        def _(step):
            to_z(step, which).start()

        to_c(level, side, which, True).start()

    send_own(0)
    y_copy(0).start()
    send_own(1)
    y_copy(1).start()

    align = align_ref[...]
    chosen = lax.broadcasted_iota(jnp.int32, (text_len, text_len), 0) == align
    place[...] = jnp.where(chosen, 1.0, 0.0).astype(jnp.bfloat16)
    edit_ids = ids_ref[1:2, :]
    row = lax.broadcasted_iota(jnp.int32, (16, text_len), 0)
    digits = jnp.where(
        row == 0,
        edit_ids >> 16,
        jnp.where(row == 1, (edit_ids >> 8) & 255, jnp.where(row == 2, edit_ids & 255, 0)),
    )
    digits = rows_by_rows(digits.astype(jnp.float32).astype(jnp.bfloat16), place[...])
    moved_ids = digits[0:1, :] * 65536.0 + digits[1:2, :] * 256.0 + digits[2:3, :]
    same = jnp.where(moved_ids == ids_ref[0:1, :].astype(jnp.float32), 1.0, 0.0)

    for i in range(4):
        text_copy(i).wait()

    def columns(pair):
        return pl.ds(pl.multiple_of(pair * wide, wide), wide)

    @pl.loop(0, pairs)
    def _(pair):
        for i in range(2):
            moved[i, :, columns(pair)] = jnp.dot(
                place[...], text[2 * i + 1, :, columns(pair)], preferred_element_type=jnp.float32
            ).astype(jnp.bfloat16)

    def pass_on(step, which):
        lev = (level + step) % tall
        arrived(index(lev, side, core), which)
        to_x(lev, which, False).start()
        to_c(lev, side, which, False).start()

    def pass_core(step, which):
        lev = (level + step) % tall
        arrived(index(lev, 1 - side, core), which)
        to_c(lev, 1 - side, which, False).start()

    def from_core(which):
        @pl.loop(0, 2 * tall)
        def _(i):
            arrived(index(i // 2, i % 2, 1 - core), which)

    @pl.loop(1, tall)
    def _(step):
        pass_on(step, 0)
        pass_core(step - 1, 0)

    pass_core(tall - 1, 0)
    own_copy(0).wait()
    own_copy(2).wait()
    y_copy(0).wait_recv()
    from_core(0)

    def head_columns(pair, i):
        return pl.ds(pl.multiple_of(pair * wide + i * HD, HD), HD)

    def joined(value):
        flat = value.astype(jnp.float32).reshape(value.shape[0] * value.shape[1], HD)
        return flat.astype(jnp.bfloat16)

    def weigh(pair):
        for i in range(PAIR):
            at = head_columns(pair, i)
            scores = rows_by_rows(joined(q_all[:, :, at]), joined(kv_all[:, 0, :, at]))
            peak = jnp.max(scores, axis=1, keepdims=True)
            weights = jnp.exp((scores - peak) * scale)
            total = jnp.sum(weights, axis=1, keepdims=True)
            probs[pair * PAIR + i] = weights.astype(jnp.bfloat16)
            totals[pair * PAIR + i] = jnp.broadcast_to(total, (2 * rows, HD))

    @pl.loop(1, tall)
    def _(step):
        pass_on(step, 1)
        pass_core(step - 1, 1)

        @pl.loop((step - 1) * pairs // (tall - 1), step * pairs // (tall - 1))
        def _(pair):
            weigh(pair)

    pass_core(tall - 1, 1)
    own_copy(1).wait()
    own_copy(3).wait()
    y_copy(1).wait_recv()
    from_core(1)

    def back_copy(which, pair):
        source, target = ((att, att_ref), (out, out_ref))[which]
        return pltpu.make_async_remote_copy(
            src_ref=source.at[other, :, columns(pair)],
            dst_ref=target.at[:, pl.ds(pl.multiple_of(mine + pair * wide, HD), wide)],
            send_sem=back_send.at[which, pair],
            recv_sem=back_recv.at[which, pair],
            device_id=(me, other),
            device_id_type=MESH,
        )

    def own_out(which, pair):
        source, target = ((att, att_ref), (out, out_ref))[which]
        return pltpu.make_async_copy(
            source.at[branch, :, columns(pair)],
            target.at[:, pl.ds(pl.multiple_of(mine + pair * wide, HD), wide)],
            own_out_sem.at[which, pair],
        )

    squares[0] = jnp.zeros((2 * rows, HD), jnp.float32)

    @pl.loop(0, pairs)
    def _(pair):
        added = squares[0]
        for i in range(PAIR):
            at = head_columns(pair, i)
            summed = jnp.dot(
                probs[pair * PAIR + i],
                joined(kv_all[:, 1, :, at]),
                preferred_element_type=jnp.float32,
            )
            rounded = (summed / totals[pair * PAIR + i]).reshape(2, rows, HD).astype(jnp.bfloat16)
            att[:, :, at] = rounded
            middle = r_all[:, :, at].astype(jnp.float32) + rounded.astype(jnp.float32)
            mid[:, :, at] = middle
            middle = middle.reshape(2 * rows, HD)
            added = added + middle * middle
        squares[0] = added
        back_copy(0, pair).start()
        own_out(0, pair).start()

    squares[0] = jnp.broadcast_to(
        jnp.sum(squares[0], axis=1, keepdims=True), (2 * rows, HD)
    )
    square_copy = pltpu.make_async_remote_copy(
        src_ref=squares.at[0],
        dst_ref=squares.at[1],
        send_sem=y_send.at[2],
        recv_sem=y_recv.at[2],
        device_id=(me, other),
        device_id_type=MESH,
    )
    square_copy.start()
    square_copy.wait_recv()
    norm = lax.rsqrt((squares[0] + squares[1]) * (1.0 / (2 * half)) + 1e-06)
    squares[2] = norm

    def text_map(query, keys):
        scores = rows_by_rows(query, keys)
        weights = jnp.exp((scores - jnp.max(scores, axis=1, keepdims=True)) * scale)
        return weights / jnp.sum(weights, axis=1, keepdims=True)

    @pl.loop(0, pairs)
    def _(pair):
        for i in range(PAIR):
            at = head_columns(pair, i)
            gain = gain_ref[:, pl.ds(pl.multiple_of(mine + pair * wide + i * HD, HD), HD)]
            middle = mid[:, :, at]
            query = middle.reshape(2 * rows, HD) * squares[2] * gain.astype(jnp.float32)
            query = query.reshape(2, rows, HD).astype(jnp.bfloat16)
            source_map = text_map(query[0], text[0, :, at])
            edit_map = text_map(query[1], moved[0, :, at])
            injected = jnp.where(same > 0.5, source_map, edit_map)
            source_out = jnp.dot(
                source_map.astype(jnp.bfloat16),
                text[2, :, at],
                preferred_element_type=jnp.float32,
            )
            edit_out = jnp.dot(
                injected.astype(jnp.bfloat16),
                moved[1, :, at],
                preferred_element_type=jnp.float32,
            )
            out[0, :, at] = (middle[0] + source_out).astype(jnp.bfloat16)
            out[1, :, at] = (middle[1] + edit_out).astype(jnp.bfloat16)
        back_copy(1, pair).start()
        own_out(1, pair).start()

    for which in range(2):

        @pl.loop(0, pairs)
        def _(pair):
            back_copy(which, pair).wait()
            own_out(which, pair).wait()

        y_copy(which).wait_send()
        to_x(level, which, True).wait_send()
        to_c(level, side, which, True).wait_send()
        to_c(level, 1 - side, which, False).wait_send()

        @pl.loop(1, tall)
        def _(step):
            lev = (level + step) % tall
            to_z(step, which).wait_send()
            to_x(lev, which, False).wait_send()
            to_c(lev, side, which, False).wait_send()
            to_c(lev, 1 - side, which, False).wait_send()

    square_copy.wait_send()


def per_device(n, queries, keys_values, residual_in, cross_gain, text_kv, prompt_ids, word_align):
    rows, width = queries.shape[1:]
    half = keys_values.shape[2]
    heads = half // HD
    pairs = heads // PAIR
    text_len = word_align.shape[0]
    keys = n * rows
    tall = n // 4
    vmem = pl.BlockSpec(memory_space=pltpu.VMEM)
    hbm = pl.BlockSpec(memory_space=pl.ANY)
    shape = jax.ShapeDtypeStruct((rows, width), jnp.bfloat16)
    bf16, f32 = jnp.bfloat16, jnp.float32
    dma = pltpu.SemaphoreType.DMA
    attended, result = pl.pallas_call(
        functools.partial(kernel, n),
        out_shape=(shape, shape),
        in_specs=[vmem, vmem, vmem, vmem, hbm, vmem, vmem],
        out_specs=(hbm, hbm),
        scratch_shapes=[
            pltpu.VMEM((2, rows, half), bf16),
            pltpu.VMEM((2, rows, half), bf16),
            pltpu.VMEM((n, 2, rows, half), bf16),
            pltpu.VMEM((4, text_len, half), bf16),
            pltpu.VMEM((2, text_len, half), bf16),
            pltpu.VMEM((text_len, text_len), bf16),
            pltpu.VMEM((heads, 2 * rows, keys), bf16),
            pltpu.VMEM((heads, 2 * rows, HD), f32),
            pltpu.VMEM((2, rows, half), bf16),
            pltpu.VMEM((2, rows, half), f32),
            pltpu.VMEM((3, 2 * rows, HD), f32),
            pltpu.VMEM((2, rows, half), bf16),
            dma((4,)),
            dma((4,)),
            dma((2, pairs)),
            dma((n, 2)),
            dma((tall, 2)),
            dma((tall, 2)),
            dma((2 * tall, 2)),
            dma((3,)),
            dma((3,)),
            dma((2, pairs)),
            dma((2, pairs)),
        ],
        compiler_params=pltpu.CompilerParams(
            collective_id=0, has_side_effects=True, vmem_limit_bytes=60 * 2**20
        ),
    )(
        queries[0],
        keys_values,
        residual_in[0],
        cross_gain[None],
        text_kv,
        prompt_ids,
        word_align[None],
    )
    return (attended[None], result[None])


def solution(mesh):
    in_specs = (
        P("branch", "seq", None),
        P(None, "seq", "branch"),
        P("branch", "seq", None),
        P(),
        P(),
        P(),
        P(),
    )
    out_specs = (P("branch", "seq", None), P("branch", "seq", None))
    return jax.shard_map(
        functools.partial(per_device, mesh.shape["seq"]),
        mesh=mesh,
        in_specs=in_specs,
        out_specs=out_specs,
        check_vma=False,
    )
```

```python
import functools
import math

import jax
import jax.numpy as jnp
from jax import lax
from jax.experimental import pallas as pl
from jax.experimental.pallas import tpu as pltpu
from jax.sharding import PartitionSpec as P

HD = 128
PAIR = 2
MESH = pl.DeviceIdType.MESH


def rows_by_rows(left, right):
    return lax.dot_general(
        left, right, (((1,), (1,)), ((), ())), preferred_element_type=jnp.float32
    )


def kernel(
    n,
    q_ref,
    kv_ref,
    res_ref,
    gain_ref,
    text_ref,
    ids_ref,
    align_ref,
    att_ref,
    out_ref,
    q_all,
    r_all,
    kv_all,
    text,
    moved,
    place,
    probs,
    totals,
    att,
    mid,
    squares,
    out,
    text_sem,
    own_sem,
    own_out_sem,
    recv_sem,
    send_up,
    send_down,
    send_x,
    send_c,
    y_send,
    y_recv,
    back_send,
    back_recv,
):
    rows = q_ref.shape[0]
    half = kv_ref.shape[2]
    heads = half // HD
    pairs = heads // PAIR
    wide = PAIR * HD
    text_len = text_ref.shape[2]
    tall = n // 4
    scale = 1.0 / math.sqrt(HD)
    me = lax.axis_index("seq")
    branch = lax.axis_index("branch")
    other = 1 - branch
    core = me % 2
    side = (me // 2) % 2
    level = me // 4
    mine = pl.multiple_of(branch * half, HD)
    theirs = pl.multiple_of(other * half, HD)

    def index(lev, sid, cor):
        return lev * 4 + sid * 2 + cor

    x_peer = index(level, 1 - side, core)
    c_peer = index(level, side, 1 - core)

    def text_copy(i):
        return pltpu.make_async_copy(
            text_ref.at[i // 2, i % 2, :, pl.ds(mine, half)], text.at[i], text_sem.at[i]
        )

    for i in range(4):
        text_copy(i).start()

    def own_copy(i):
        if i == 0:
            return pltpu.make_async_copy(
                q_ref.at[:, pl.ds(mine, half)], q_all.at[branch], own_sem.at[0]
            )
        if i == 1:
            return pltpu.make_async_copy(
                res_ref.at[:, pl.ds(mine, half)], r_all.at[branch], own_sem.at[1]
            )
        return pltpu.make_async_copy(kv_ref.at[i - 2], kv_all.at[me, i - 2], own_sem.at[i])

    for i in range(4):
        own_copy(i).start()

    barrier = pltpu.get_barrier_semaphore()

    def greet(seq, bra):
        pl.semaphore_signal(barrier, inc=1, device_id=(seq, bra), device_id_type=MESH)

    has_above = level + 1 < tall
    has_below = level > 0
    above = index((level + 1) % tall, side, core)
    below = index((level + tall - 1) % tall, side, core)

    @pl.when(has_above)
    def _():
        greet(above, branch)

    @pl.when(has_below)
    def _():
        greet(below, branch)

    greet(x_peer, branch)
    greet(c_peer, branch)
    greet(me, other)
    pl.semaphore_wait(barrier, 3 + has_above.astype(jnp.int32) + has_below.astype(jnp.int32))

    def kv_copy(source, origin, which, peer, sem):
        return pltpu.make_async_remote_copy(
            src_ref=source,
            dst_ref=kv_all.at[origin, which],
            send_sem=sem,
            recv_sem=recv_sem.at[origin, which],
            device_id=(peer, branch),
            device_id_type=MESH,
        )

    def to_above(lev, which, own):
        origin = index(lev, side, core)
        source = kv_ref.at[which] if own else kv_all.at[origin, which]
        return kv_copy(source, origin, which, above, send_up.at[lev, which])

    def to_below(lev, which, own):
        origin = index(lev, side, core)
        source = kv_ref.at[which] if own else kv_all.at[origin, which]
        return kv_copy(source, origin, which, below, send_down.at[lev, which])

    def to_x(lev, which, own):
        origin = index(lev, side, core)
        source = kv_ref.at[which] if own else kv_all.at[origin, which]
        return kv_copy(source, origin, which, x_peer, send_x.at[lev, which])

    def to_c(lev, sid, which, own):
        origin = index(lev, sid, core)
        source = kv_ref.at[which] if own else kv_all.at[origin, which]
        return kv_copy(source, origin, which, c_peer, send_c.at[lev * 2 + sid, which])

    def arrived(origin, which):
        pltpu.make_async_remote_copy(
            src_ref=kv_all.at[origin, which],
            dst_ref=kv_all.at[origin, which],
            send_sem=send_x.at[0, which],
            recv_sem=recv_sem.at[origin, which],
            device_id=(x_peer, branch),
            device_id_type=MESH,
        ).wait_recv()

    def y_copy(i):
        source, target = ((q_ref, q_all), (res_ref, r_all))[i]
        return pltpu.make_async_remote_copy(
            src_ref=source.at[:, pl.ds(theirs, half)],
            dst_ref=target.at[branch],
            send_sem=y_send.at[i],
            recv_sem=y_recv.at[i],
            device_id=(me, other),
            device_id_type=MESH,
        )

    def send_own(which):
        to_x(level, which, True).start()

        @pl.when(has_above)
        def _():
            to_above(level, which, True).start()

        @pl.when(has_below)
        def _():
            to_below(level, which, True).start()

        to_c(level, side, which, True).start()

    send_own(0)
    y_copy(0).start()
    send_own(1)
    y_copy(1).start()

    align = align_ref[...]
    chosen = lax.broadcasted_iota(jnp.int32, (text_len, text_len), 0) == align
    place[...] = jnp.where(chosen, 1.0, 0.0).astype(jnp.bfloat16)
    edit_ids = ids_ref[1:2, :]
    row = lax.broadcasted_iota(jnp.int32, (16, text_len), 0)
    digits = jnp.where(
        row == 0,
        edit_ids >> 16,
        jnp.where(row == 1, (edit_ids >> 8) & 255, jnp.where(row == 2, edit_ids & 255, 0)),
    )
    digits = rows_by_rows(digits.astype(jnp.float32).astype(jnp.bfloat16), place[...])
    moved_ids = digits[0:1, :] * 65536.0 + digits[1:2, :] * 256.0 + digits[2:3, :]
    same = jnp.where(moved_ids == ids_ref[0:1, :].astype(jnp.float32), 1.0, 0.0)

    for i in range(4):
        text_copy(i).wait()

    def columns(pair):
        return pl.ds(pl.multiple_of(pair * wide, wide), wide)

    def move(pair):
        for i in range(2):
            moved[i, :, columns(pair)] = jnp.dot(
                place[...], text[2 * i + 1, :, columns(pair)], preferred_element_type=jnp.float32
            ).astype(jnp.bfloat16)

    def pass_on(step, which):
        low, high = level - step, level + step

        @pl.when(low >= 0)
        def _():
            arrived(index(low, side, core), which)

            @pl.when(has_above)
            def _():
                to_above(low, which, False).start()

            to_x(low, which, False).start()
            to_c(low, side, which, False).start()

        @pl.when(high < tall)
        def _():
            arrived(index(high, side, core), which)

            @pl.when(has_below)
            def _():
                to_below(high, which, False).start()

            to_x(high, which, False).start()
            to_c(high, side, which, False).start()

    def across(lev, which):
        arrived(index(lev, 1 - side, core), which)
        to_c(lev, 1 - side, which, False).start()

    def pass_core(step, which):
        low, high = level - step, level + step

        @pl.when(low >= 0)
        def _():
            across(low, which)

        @pl.when(high < tall)
        def _():
            across(high, which)

    def from_core(which):
        @pl.loop(0, 2 * tall)
        def _(i):
            arrived(index(i // 2, i % 2, 1 - core), which)

    @pl.loop(1, tall)
    def _(step):
        pass_on(step, 0)

        @pl.when(step == 1)
        def _():
            across(level, 0)

        @pl.when(step > 1)
        def _():
            pass_core(step - 1, 0)

        @pl.loop((step - 1) * pairs // (tall - 1), step * pairs // (tall - 1))
        def _(pair):
            move(pair)

    pass_core(tall - 1, 0)
    own_copy(0).wait()
    own_copy(2).wait()
    y_copy(0).wait_recv()
    from_core(0)

    def head_columns(pair, i):
        return pl.ds(pl.multiple_of(pair * wide + i * HD, HD), HD)

    def joined(value):
        flat = value.astype(jnp.float32).reshape(value.shape[0] * value.shape[1], HD)
        return flat.astype(jnp.bfloat16)

    def weigh(pair):
        for i in range(PAIR):
            at = head_columns(pair, i)
            scores = rows_by_rows(joined(q_all[:, :, at]), joined(kv_all[:, 0, :, at]))
            peak = jnp.max(scores, axis=1, keepdims=True)
            weights = jnp.exp((scores - peak) * scale)
            total = jnp.sum(weights, axis=1, keepdims=True)
            probs[pair * PAIR + i] = weights.astype(jnp.bfloat16)
            totals[pair * PAIR + i] = jnp.broadcast_to(total, (2 * rows, HD))

    @pl.loop(1, tall)
    def _(step):
        pass_on(step, 1)

        @pl.when(step == 1)
        def _():
            across(level, 1)

        @pl.when(step > 1)
        def _():
            pass_core(step - 1, 1)

        @pl.loop((step - 1) * pairs // (tall - 1), step * pairs // (tall - 1))
        def _(pair):
            weigh(pair)

    pass_core(tall - 1, 1)
    own_copy(1).wait()
    own_copy(3).wait()
    y_copy(1).wait_recv()
    from_core(1)

    def back_copy(which, pair):
        source, target = ((att, att_ref), (out, out_ref))[which]
        return pltpu.make_async_remote_copy(
            src_ref=source.at[other, :, columns(pair)],
            dst_ref=target.at[:, pl.ds(pl.multiple_of(mine + pair * wide, HD), wide)],
            send_sem=back_send.at[which, pair],
            recv_sem=back_recv.at[which, pair],
            device_id=(me, other),
            device_id_type=MESH,
        )

    def own_out(which, pair):
        source, target = ((att, att_ref), (out, out_ref))[which]
        return pltpu.make_async_copy(
            source.at[branch, :, columns(pair)],
            target.at[:, pl.ds(pl.multiple_of(mine + pair * wide, HD), wide)],
            own_out_sem.at[which, pair],
        )

    squares[0] = jnp.zeros((2 * rows, HD), jnp.float32)

    @pl.loop(0, pairs)
    def _(pair):
        added = squares[0]
        for i in range(PAIR):
            at = head_columns(pair, i)
            summed = jnp.dot(
                probs[pair * PAIR + i],
                joined(kv_all[:, 1, :, at]),
                preferred_element_type=jnp.float32,
            )
            rounded = (summed / totals[pair * PAIR + i]).reshape(2, rows, HD).astype(jnp.bfloat16)
            att[:, :, at] = rounded
            middle = r_all[:, :, at].astype(jnp.float32) + rounded.astype(jnp.float32)
            mid[:, :, at] = middle
            middle = middle.reshape(2 * rows, HD)
            added = added + middle * middle
        squares[0] = added
        back_copy(0, pair).start()
        own_out(0, pair).start()

    squares[0] = jnp.broadcast_to(
        jnp.sum(squares[0], axis=1, keepdims=True), (2 * rows, HD)
    )
    square_copy = pltpu.make_async_remote_copy(
        src_ref=squares.at[0],
        dst_ref=squares.at[1],
        send_sem=y_send.at[2],
        recv_sem=y_recv.at[2],
        device_id=(me, other),
        device_id_type=MESH,
    )
    square_copy.start()
    square_copy.wait_recv()
    norm = lax.rsqrt((squares[0] + squares[1]) * (1.0 / (2 * half)) + 1e-06)
    squares[2] = norm

    def text_map(query, keys):
        scores = rows_by_rows(query, keys)
        weights = jnp.exp((scores - jnp.max(scores, axis=1, keepdims=True)) * scale)
        return weights / jnp.sum(weights, axis=1, keepdims=True)

    @pl.loop(0, pairs)
    def _(pair):
        for i in range(PAIR):
            at = head_columns(pair, i)
            gain = gain_ref[:, pl.ds(pl.multiple_of(mine + pair * wide + i * HD, HD), HD)]
            middle = mid[:, :, at]
            query = middle.reshape(2 * rows, HD) * squares[2] * gain.astype(jnp.float32)
            query = query.reshape(2, rows, HD).astype(jnp.bfloat16)
            source_map = text_map(query[0], text[0, :, at])
            edit_map = text_map(query[1], moved[0, :, at])
            injected = jnp.where(same > 0.5, source_map, edit_map)
            source_out = jnp.dot(
                source_map.astype(jnp.bfloat16),
                text[2, :, at],
                preferred_element_type=jnp.float32,
            )
            edit_out = jnp.dot(
                injected.astype(jnp.bfloat16),
                moved[1, :, at],
                preferred_element_type=jnp.float32,
            )
            out[0, :, at] = (middle[0] + source_out).astype(jnp.bfloat16)
            out[1, :, at] = (middle[1] + edit_out).astype(jnp.bfloat16)
        back_copy(1, pair).start()
        own_out(1, pair).start()

    for which in range(2):

        @pl.loop(0, pairs)
        def _(pair):
            back_copy(which, pair).wait()
            own_out(which, pair).wait()

        y_copy(which).wait_send()

        @pl.loop(0, tall)
        def _(lev):
            to_x(lev, which, False).wait_send()
            to_c(lev, 0, which, False).wait_send()
            to_c(lev, 1, which, False).wait_send()

            @pl.when(jnp.logical_and(has_above, lev <= level))
            def _():
                to_above(lev, which, False).wait_send()

            @pl.when(jnp.logical_and(has_below, lev >= level))
            def _():
                to_below(lev, which, False).wait_send()

    square_copy.wait_send()


def copy_out(att_in, out_in, att_ref, out_ref, sem):
    half = att_in.shape[1] // 2
    copies = []
    for i, (source, target) in enumerate(((att_in, att_ref), (out_in, out_ref))):
        for j in range(2):
            at = pl.ds(j * half, half)
            copies.append(
                pltpu.make_async_copy(source.at[:, at], target.at[:, at], sem.at[2 * i + j])
            )
    for copy in copies:
        copy.start()
    for copy in copies:
        copy.wait()


def per_device(n, queries, keys_values, residual_in, cross_gain, text_kv, prompt_ids, word_align):
    rows, width = queries.shape[1:]
    half = keys_values.shape[2]
    heads = half // HD
    pairs = heads // PAIR
    text_len = word_align.shape[0]
    keys = n * rows
    tall = n // 4
    vmem = pl.BlockSpec(memory_space=pltpu.VMEM)
    hbm = pl.BlockSpec(memory_space=pl.ANY)
    shape = jax.ShapeDtypeStruct((rows, width), jnp.bfloat16)
    bf16, f32 = jnp.bfloat16, jnp.float32
    dma = pltpu.SemaphoreType.DMA
    attended, result = pl.pallas_call(
        functools.partial(kernel, n),
        out_shape=(shape, shape),
        in_specs=[vmem, vmem, vmem, vmem, hbm, vmem, vmem],
        out_specs=(hbm, hbm),
        scratch_shapes=[
            pltpu.VMEM((2, rows, half), bf16),
            pltpu.VMEM((2, rows, half), bf16),
            pltpu.VMEM((n, 2, rows, half), bf16),
            pltpu.VMEM((4, text_len, half), bf16),
            pltpu.VMEM((2, text_len, half), bf16),
            pltpu.VMEM((text_len, text_len), bf16),
            pltpu.VMEM((heads, 2 * rows, keys), bf16),
            pltpu.VMEM((heads, 2 * rows, HD), f32),
            pltpu.VMEM((2, rows, half), bf16),
            pltpu.VMEM((2, rows, half), f32),
            pltpu.VMEM((3, 2 * rows, HD), f32),
            pltpu.VMEM((2, rows, half), bf16),
            dma((4,)),
            dma((4,)),
            dma((2, pairs)),
            dma((n, 2)),
            dma((tall, 2)),
            dma((tall, 2)),
            dma((tall, 2)),
            dma((2 * tall, 2)),
            dma((3,)),
            dma((3,)),
            dma((2, pairs)),
            dma((2, pairs)),
        ],
        compiler_params=pltpu.CompilerParams(
            collective_id=0, has_side_effects=True, vmem_limit_bytes=60 * 2**20
        ),
    )(
        queries[0],
        keys_values,
        residual_in[0],
        cross_gain[None],
        text_kv,
        prompt_ids,
        word_align[None],
    )
    attended, result = pl.pallas_call(
        copy_out,
        out_shape=(shape, shape),
        in_specs=[hbm, hbm],
        out_specs=(hbm, hbm),
        scratch_shapes=[dma((4,))],
    )(attended, result)
    return (attended[None], result[None])


def solution(mesh):
    in_specs = (
        P("branch", "seq", None),
        P(None, "seq", "branch"),
        P("branch", "seq", None),
        P(),
        P(),
        P(),
        P(),
    )
    out_specs = (P("branch", "seq", None), P("branch", "seq", None))
    return jax.shard_map(
        functools.partial(per_device, mesh.shape["seq"]),
        mesh=mesh,
        in_specs=in_specs,
        out_specs=out_specs,
        check_vma=False,
    )
```

```python
import functools
import math

import jax
import jax.numpy as jnp
from jax import lax
from jax.experimental import pallas as pl
from jax.experimental.pallas import tpu as pltpu
from jax.sharding import PartitionSpec as P

HD = 128
PAIR = 2
MESH = pl.DeviceIdType.MESH


def rows_by_rows(left, right):
    return lax.dot_general(
        left, right, (((1,), (1,)), ((), ())), preferred_element_type=jnp.float32
    )


def kernel(
    n,
    q_ref,
    kv_ref,
    res_ref,
    gain_ref,
    text_ref,
    ids_ref,
    align_ref,
    att_ref,
    out_ref,
    q_all,
    r_all,
    kv_all,
    text,
    moved,
    place,
    probs,
    totals,
    att,
    mid,
    squares,
    out,
    text_sem,
    own_sem,
    own_out_sem,
    recv_sem,
    send_up,
    send_down,
    send_x,
    send_c,
    relay_sem,
    y_send,
    y_recv,
    back_send,
    back_recv,
):
    rows = q_ref.shape[0]
    half = kv_ref.shape[2]
    heads = half // HD
    pairs = heads // PAIR
    wide = PAIR * HD
    grouped = heads // 2 if heads % 2 == 0 else heads
    groups = heads // grouped
    text_len = text_ref.shape[2]
    tall = n // 4
    scale = 1.0 / math.sqrt(HD)
    me = lax.axis_index("seq")
    branch = lax.axis_index("branch")
    other = 1 - branch
    core = me % 2
    side = (me // 2) % 2
    level = me // 4
    mine = pl.multiple_of(branch * half, HD)
    theirs = pl.multiple_of(other * half, HD)

    def index(lev, sid, cor):
        return lev * 4 + sid * 2 + cor

    x_peer = index(level, 1 - side, core)
    c_peer = index(level, side, 1 - core)

    def text_copy(i):
        return pltpu.make_async_copy(
            text_ref.at[i // 2, i % 2, :, pl.ds(mine, half)], text.at[i], text_sem.at[i]
        )

    for i in range(4):
        text_copy(i).start()

    def own_copy(i):
        if i == 0:
            return pltpu.make_async_copy(
                q_ref.at[:, pl.ds(mine, half)], q_all.at[branch], own_sem.at[0]
            )
        if i == 1:
            return pltpu.make_async_copy(
                res_ref.at[:, pl.ds(mine, half)], r_all.at[branch], own_sem.at[1]
            )
        return pltpu.make_async_copy(kv_ref.at[i - 2], kv_all.at[me, i - 2], own_sem.at[i])

    for i in range(4):
        own_copy(i).start()

    barrier = pltpu.get_barrier_semaphore()

    def greet(seq, bra):
        pl.semaphore_signal(barrier, inc=1, device_id=(seq, bra), device_id_type=MESH)

    has_above = level + 1 < tall
    has_below = level > 0
    above = index((level + 1) % tall, side, core)
    below = index((level + tall - 1) % tall, side, core)

    @pl.when(has_above)
    def _():
        greet(above, branch)

    @pl.when(has_below)
    def _():
        greet(below, branch)

    greet(x_peer, branch)
    greet(c_peer, branch)
    greet(me, other)
    pl.semaphore_wait(barrier, 3 + has_above.astype(jnp.int32) + has_below.astype(jnp.int32))

    def kv_copy(source, origin, which, peer, sem):
        return pltpu.make_async_remote_copy(
            src_ref=source,
            dst_ref=kv_all.at[origin, which],
            send_sem=sem,
            recv_sem=recv_sem.at[origin, which],
            device_id=(peer, branch),
            device_id_type=MESH,
        )

    def to_above(lev, which, own):
        origin = index(lev, side, core)
        source = kv_ref.at[which] if own else kv_all.at[origin, which]
        return kv_copy(source, origin, which, above, send_up.at[lev, which])

    def to_below(lev, which, own):
        origin = index(lev, side, core)
        source = kv_ref.at[which] if own else kv_all.at[origin, which]
        return kv_copy(source, origin, which, below, send_down.at[lev, which])

    def to_x(lev, which, own):
        origin = index(lev, side, core)
        source = kv_ref.at[which] if own else kv_all.at[origin, which]
        return kv_copy(source, origin, which, x_peer, send_x.at[lev, which])

    def to_c(lev, sid, which, own):
        origin = index(lev, sid, core)
        source = kv_ref.at[which] if own else kv_all.at[origin, which]
        return kv_copy(source, origin, which, c_peer, send_c.at[lev * 2 + sid, which])

    def arrived(origin, which):
        pltpu.make_async_remote_copy(
            src_ref=kv_all.at[origin, which],
            dst_ref=kv_all.at[origin, which],
            send_sem=send_x.at[0, which],
            recv_sem=recv_sem.at[origin, which],
            device_id=(x_peer, branch),
            device_id_type=MESH,
        ).wait_recv()

    def y_copy(i):
        source, target = ((q_ref, q_all), (res_ref, r_all))[i]
        return pltpu.make_async_remote_copy(
            src_ref=source.at[:, pl.ds(theirs, half)],
            dst_ref=target.at[branch],
            send_sem=y_send.at[i],
            recv_sem=y_recv.at[i],
            device_id=(me, other),
            device_id_type=MESH,
        )

    def send_own(which):
        to_x(level, which, True).start()

        @pl.when(has_above)
        def _():
            to_above(level, which, True).start()

        @pl.when(has_below)
        def _():
            to_below(level, which, True).start()

        to_c(level, side, which, True).start()

    send_own(0)
    y_copy(0).start()
    send_own(1)
    y_copy(1).start()

    align = align_ref[...]
    chosen = lax.broadcasted_iota(jnp.int32, (text_len, text_len), 0) == align
    place[...] = jnp.where(chosen, 1.0, 0.0).astype(jnp.bfloat16)
    edit_ids = ids_ref[1:2, :]
    row = lax.broadcasted_iota(jnp.int32, (16, text_len), 0)
    digits = jnp.where(
        row == 0,
        edit_ids >> 16,
        jnp.where(row == 1, (edit_ids >> 8) & 255, jnp.where(row == 2, edit_ids & 255, 0)),
    )
    digits = rows_by_rows(digits.astype(jnp.float32).astype(jnp.bfloat16), place[...])
    moved_ids = digits[0:1, :] * 65536.0 + digits[1:2, :] * 256.0 + digits[2:3, :]
    same = jnp.where(moved_ids == ids_ref[0:1, :].astype(jnp.float32), 1.0, 0.0)

    for i in range(4):
        text_copy(i).wait()

    def columns(pair):
        return pl.ds(pl.multiple_of(pair * wide, wide), wide)

    def move(pair):
        for i in range(2):
            moved[i, :, columns(pair)] = jnp.dot(
                place[...], text[2 * i + 1, :, columns(pair)], preferred_element_type=jnp.float32
            ).astype(jnp.bfloat16)

    paired = level + 1 - 2 * (level % 2)
    relieved = paired < tall

    def relayed(lev, which):
        return jnp.logical_and(lev == paired, relieved) if which == 1 else False

    def forward_x(lev, which):
        if which == 0:
            to_x(lev, which, False).start()
        else:

            @pl.when(jnp.logical_not(relayed(lev, which)))
            def _():
                to_x(lev, which, False).start()

    def to_paired():
        origin = index(level, 1 - side, core)
        peer = index(lax.rem(paired, tall), side, core)
        return kv_copy(kv_all.at[origin, 1], origin, 1, peer, relay_sem.at[0])

    def pass_on(step, which):
        low, high = level - step, level + step

        @pl.when(low >= 0)
        def _():
            arrived(index(low, side, core), which)

            @pl.when(has_above)
            def _():
                to_above(low, which, False).start()

            forward_x(low, which)
            to_c(low, side, which, False).start()

        @pl.when(high < tall)
        def _():
            arrived(index(high, side, core), which)

            @pl.when(has_below)
            def _():
                to_below(high, which, False).start()

            forward_x(high, which)
            to_c(high, side, which, False).start()

    def across(lev, which):
        arrived(index(lev, 1 - side, core), which)
        if which == 1 and lev is level:

            @pl.when(relieved)
            def _():
                to_paired().start()

        to_c(lev, 1 - side, which, False).start()

    def pass_core(step, which):
        low, high = level - step, level + step

        @pl.when(low >= 0)
        def _():
            across(low, which)

        @pl.when(high < tall)
        def _():
            across(high, which)

    def from_core(which):
        @pl.loop(0, 2 * tall)
        def _(i):
            arrived(index(i // 2, i % 2, 1 - core), which)

    def moves(step):
        @pl.loop((step - 1) * pairs // (tall - 1), step * pairs // (tall - 1))
        def _(pair):
            move(pair)

    def pass_core_or_own(step, which):
        @pl.when(step == 0)
        def _():
            across(level, which)

        @pl.when(step > 0)
        def _():
            pass_core(step, which)

    pass_on(1, 0)
    across(level, 0)
    moves(1)

    @pl.loop(2, tall)
    def _(step):
        pass_on(step, 0)
        pass_core(step - 1, 0)
        pass_on(step - 1, 1)
        pass_core_or_own(step - 2, 1)
        moves(step)

    pass_core(tall - 1, 0)
    own_copy(0).wait()
    own_copy(2).wait()
    y_copy(0).wait_recv()
    from_core(0)

    def head_columns(pair, i):
        return pl.ds(pl.multiple_of(pair * wide + i * HD, HD), HD)

    def joined(value):
        flat = value.astype(jnp.float32).reshape(value.shape[0] * value.shape[1], HD)
        return flat.astype(jnp.bfloat16)

    def weigh(group):
        for i in range(grouped):
            head = group * grouped + i
            at = pl.ds(pl.multiple_of(head * HD, HD), HD)
            scores = rows_by_rows(joined(q_all[:, :, at]), joined(kv_all[:, 0, :, at]))
            peak = jnp.max(scores, axis=1, keepdims=True)
            weights = jnp.exp((scores - peak) * scale)
            total = jnp.sum(weights, axis=1, keepdims=True)
            probs[head] = weights.astype(jnp.bfloat16)
            totals[head] = jnp.broadcast_to(total, (2 * rows, HD))

    weigh(0)
    pass_on(tall - 1, 1)
    pass_core_or_own(tall - 2, 1)

    @pl.loop(1, groups)
    def _(group):
        weigh(group)

    pass_core(tall - 1, 1)
    own_copy(1).wait()
    own_copy(3).wait()
    y_copy(1).wait_recv()
    from_core(1)

    def span(which, part):
        size = (grouped * HD, wide)[which]
        return pl.multiple_of(part * size, HD), size

    def back_copy(which, part):
        source, target = ((att, att_ref), (out, out_ref))[which]
        start, size = span(which, part)
        return pltpu.make_async_remote_copy(
            src_ref=source.at[other, :, pl.ds(start, size)],
            dst_ref=target.at[:, pl.ds(pl.multiple_of(mine + start, HD), size)],
            send_sem=back_send.at[which, part],
            recv_sem=back_recv.at[which, part],
            device_id=(me, other),
            device_id_type=MESH,
        )

    def own_out(which, part):
        source, target = ((att, att_ref), (out, out_ref))[which]
        start, size = span(which, part)
        return pltpu.make_async_copy(
            source.at[branch, :, pl.ds(start, size)],
            target.at[:, pl.ds(pl.multiple_of(mine + start, HD), size)],
            own_out_sem.at[which, part],
        )

    squares[0] = jnp.zeros((2 * rows, HD), jnp.float32)

    @pl.loop(0, groups)
    def _(group):
        added = squares[0]
        for i in range(grouped):
            head = group * grouped + i
            at = pl.ds(pl.multiple_of(head * HD, HD), HD)
            summed = jnp.dot(
                probs[head],
                joined(kv_all[:, 1, :, at]),
                preferred_element_type=jnp.float32,
            )
            rounded = (summed / totals[head]).reshape(2, rows, HD).astype(jnp.bfloat16)
            att[:, :, at] = rounded
            middle = r_all[:, :, at].astype(jnp.float32) + rounded.astype(jnp.float32)
            mid[:, :, at] = middle
            middle = middle.reshape(2 * rows, HD)
            added = added + middle * middle
        squares[0] = added
        back_copy(0, group).start()
        own_out(0, group).start()

    squares[0] = jnp.broadcast_to(
        jnp.sum(squares[0], axis=1, keepdims=True), (2 * rows, HD)
    )
    square_copy = pltpu.make_async_remote_copy(
        src_ref=squares.at[0],
        dst_ref=squares.at[1],
        send_sem=y_send.at[2],
        recv_sem=y_recv.at[2],
        device_id=(me, other),
        device_id_type=MESH,
    )
    square_copy.start()
    square_copy.wait_recv()
    norm = lax.rsqrt((squares[0] + squares[1]) * (1.0 / (2 * half)) + 1e-06)
    squares[2] = norm

    def text_map(query, keys):
        scores = rows_by_rows(query, keys)
        weights = jnp.exp((scores - jnp.max(scores, axis=1, keepdims=True)) * scale)
        return weights / jnp.sum(weights, axis=1, keepdims=True)

    @pl.loop(0, pairs)
    def _(pair):
        for i in range(PAIR):
            at = head_columns(pair, i)
            gain = gain_ref[:, pl.ds(pl.multiple_of(mine + pair * wide + i * HD, HD), HD)]
            middle = mid[:, :, at]
            query = middle.reshape(2 * rows, HD) * squares[2] * gain.astype(jnp.float32)
            query = query.reshape(2, rows, HD).astype(jnp.bfloat16)
            source_map = text_map(query[0], text[0, :, at])
            edit_map = text_map(query[1], moved[0, :, at])
            injected = jnp.where(same > 0.5, source_map, edit_map)
            source_out = jnp.dot(
                source_map.astype(jnp.bfloat16),
                text[2, :, at],
                preferred_element_type=jnp.float32,
            )
            edit_out = jnp.dot(
                injected.astype(jnp.bfloat16),
                moved[1, :, at],
                preferred_element_type=jnp.float32,
            )
            out[0, :, at] = (middle[0] + source_out).astype(jnp.bfloat16)
            out[1, :, at] = (middle[1] + edit_out).astype(jnp.bfloat16)
        back_copy(1, pair).start()
        own_out(1, pair).start()

    for which in range(2):

        @pl.loop(0, (groups, pairs)[which])
        def _(part):
            back_copy(which, part).wait()
            own_out(which, part).wait()

        y_copy(which).wait_send()

        @pl.loop(0, tall)
        def _(lev):
            if which == 0:
                to_x(lev, which, False).wait_send()
            else:

                @pl.when(jnp.logical_not(relayed(lev, which)))
                def _():
                    to_x(lev, which, False).wait_send()

            to_c(lev, 0, which, False).wait_send()
            to_c(lev, 1, which, False).wait_send()

            @pl.when(jnp.logical_and(has_above, lev <= level))
            def _():
                to_above(lev, which, False).wait_send()

            @pl.when(jnp.logical_and(has_below, lev >= level))
            def _():
                to_below(lev, which, False).wait_send()

    @pl.when(relieved)
    def _():
        to_paired().wait_send()

    square_copy.wait_send()


def copy_out(att_in, out_in, att_ref, out_ref):
    att_ref[...] = att_in[...]
    out_ref[...] = out_in[...]


def per_device(n, queries, keys_values, residual_in, cross_gain, text_kv, prompt_ids, word_align):
    rows, width = queries.shape[1:]
    half = keys_values.shape[2]
    heads = half // HD
    pairs = heads // PAIR
    text_len = word_align.shape[0]
    keys = n * rows
    tall = n // 4
    vmem = pl.BlockSpec(memory_space=pltpu.VMEM)
    hbm = pl.BlockSpec(memory_space=pl.ANY)
    shape = jax.ShapeDtypeStruct((rows, width), jnp.bfloat16)
    bf16, f32 = jnp.bfloat16, jnp.float32
    dma = pltpu.SemaphoreType.DMA
    attended, result = pl.pallas_call(
        functools.partial(kernel, n),
        out_shape=(shape, shape),
        in_specs=[vmem, vmem, vmem, vmem, hbm, vmem, vmem],
        out_specs=(hbm, hbm),
        scratch_shapes=[
            pltpu.VMEM((2, rows, half), bf16),
            pltpu.VMEM((2, rows, half), bf16),
            pltpu.VMEM((n, 2, rows, half), bf16),
            pltpu.VMEM((4, text_len, half), bf16),
            pltpu.VMEM((2, text_len, half), bf16),
            pltpu.VMEM((text_len, text_len), bf16),
            pltpu.VMEM((heads, 2 * rows, keys), bf16),
            pltpu.VMEM((heads, 2 * rows, HD), f32),
            pltpu.VMEM((2, rows, half), bf16),
            pltpu.VMEM((2, rows, half), f32),
            pltpu.VMEM((3, 2 * rows, HD), f32),
            pltpu.VMEM((2, rows, half), bf16),
            dma((4,)),
            dma((4,)),
            dma((2, pairs)),
            dma((n, 2)),
            dma((tall, 2)),
            dma((tall, 2)),
            dma((tall, 2)),
            dma((2 * tall, 2)),
            dma((1,)),
            dma((3,)),
            dma((3,)),
            dma((2, pairs)),
            dma((2, pairs)),
        ],
        compiler_params=pltpu.CompilerParams(
            collective_id=0, has_side_effects=True, vmem_limit_bytes=60 * 2**20
        ),
    )(
        queries[0],
        keys_values,
        residual_in[0],
        cross_gain[None],
        text_kv,
        prompt_ids,
        word_align[None],
    )
    attended, result = pl.pallas_call(
        copy_out,
        out_shape=(shape, shape),
        in_specs=[vmem, vmem],
        out_specs=(vmem, vmem),
    )(attended, result)
    return (attended[None], result[None])


def solution(mesh):
    in_specs = (
        P("branch", "seq", None),
        P(None, "seq", "branch"),
        P("branch", "seq", None),
        P(),
        P(),
        P(),
        P(),
    )
    out_specs = (P("branch", "seq", None), P("branch", "seq", None))
    return jax.shard_map(
        functools.partial(per_device, mesh.shape["seq"]),
        mesh=mesh,
        in_specs=in_specs,
        out_specs=out_specs,
        check_vma=False,
    )
```

```python
import functools
import math

import jax
import jax.numpy as jnp
from jax import lax
from jax.experimental import pallas as pl
from jax.experimental.pallas import tpu as pltpu
from jax.sharding import PartitionSpec as P

HD = 128
PAIR = 2
MESH = pl.DeviceIdType.MESH


def rows_by_rows(left, right):
    return lax.dot_general(
        left, right, (((1,), (1,)), ((), ())), preferred_element_type=jnp.float32
    )


def kernel(
    n,
    q_ref,
    kv_ref,
    res_ref,
    gain_ref,
    text_ref,
    ids_ref,
    align_ref,
    att_ref,
    out_ref,
    q_all,
    r_all,
    kv_all,
    text,
    moved,
    place,
    probs,
    totals,
    att,
    mid,
    squares,
    partial,
    out,
    text_sem,
    own_sem,
    own_out_sem,
    recv_sem,
    send_up,
    send_down,
    send_x,
    send_c,
    relay_sem,
    y_send,
    y_recv,
    back_send,
    back_recv,
):
    rows = q_ref.shape[0]
    half = kv_ref.shape[2]
    heads = half // HD
    pairs = heads // PAIR
    wide = PAIR * HD
    grouped = heads // 2 if heads % 2 == 0 else heads
    groups = heads // grouped
    part = grouped * HD
    classes = 2 * groups
    text_len = text_ref.shape[2]
    tall = n // 4
    scale = 1.0 / math.sqrt(HD)
    me = lax.axis_index("seq")
    branch = lax.axis_index("branch")
    other = 1 - branch
    core = me % 2
    side = (me // 2) % 2
    level = me // 4
    mine = pl.multiple_of(branch * half, HD)
    theirs = pl.multiple_of(other * half, HD)

    def index(lev, sid, cor):
        return lev * 4 + sid * 2 + cor

    def own_kv(which):
        return kv_ref.at[which // groups, :, pl.ds(which % groups * part, part)]

    x_peer = index(level, 1 - side, core)
    c_peer = index(level, side, 1 - core)

    def text_copy(i):
        return pltpu.make_async_copy(
            text_ref.at[i // 2, i % 2, :, pl.ds(mine, half)], text.at[i], text_sem.at[i]
        )

    for i in range(4):
        text_copy(i).start()

    def own_copy(i):
        if i == 0:
            return pltpu.make_async_copy(
                q_ref.at[:, pl.ds(mine, half)], q_all.at[branch], own_sem.at[0]
            )
        if i == 1:
            return pltpu.make_async_copy(
                res_ref.at[:, pl.ds(mine, half)], r_all.at[branch], own_sem.at[1]
            )
        return pltpu.make_async_copy(own_kv(i - 2), kv_all.at[me, i - 2], own_sem.at[i])

    for i in range(2 + classes):
        own_copy(i).start()

    barrier = pltpu.get_barrier_semaphore()

    def greet(seq, bra):
        pl.semaphore_signal(barrier, inc=1, device_id=(seq, bra), device_id_type=MESH)

    has_above = level + 1 < tall
    has_below = level > 0
    above = index((level + 1) % tall, side, core)
    below = index((level + tall - 1) % tall, side, core)

    @pl.when(has_above)
    def _():
        greet(above, branch)

    @pl.when(has_below)
    def _():
        greet(below, branch)

    greet(x_peer, branch)
    greet(c_peer, branch)
    greet(me, other)
    pl.semaphore_wait(barrier, 3 + has_above.astype(jnp.int32) + has_below.astype(jnp.int32))

    def kv_copy(source, origin, which, peer, sem):
        return pltpu.make_async_remote_copy(
            src_ref=source,
            dst_ref=kv_all.at[origin, which],
            send_sem=sem,
            recv_sem=recv_sem.at[origin, which],
            device_id=(peer, branch),
            device_id_type=MESH,
        )

    def to_above(lev, which, own):
        origin = index(lev, side, core)
        source = own_kv(which) if own else kv_all.at[origin, which]
        return kv_copy(source, origin, which, above, send_up.at[lev, which])

    def to_below(lev, which, own):
        origin = index(lev, side, core)
        source = own_kv(which) if own else kv_all.at[origin, which]
        return kv_copy(source, origin, which, below, send_down.at[lev, which])

    def to_x(lev, which, own):
        origin = index(lev, side, core)
        source = own_kv(which) if own else kv_all.at[origin, which]
        return kv_copy(source, origin, which, x_peer, send_x.at[lev, which])

    def to_c(lev, sid, which, own):
        origin = index(lev, sid, core)
        source = own_kv(which) if own else kv_all.at[origin, which]
        return kv_copy(source, origin, which, c_peer, send_c.at[lev * 2 + sid, which])

    def arrived(origin, which):
        pltpu.make_async_remote_copy(
            src_ref=kv_all.at[origin, which],
            dst_ref=kv_all.at[origin, which],
            send_sem=send_x.at[0, which],
            recv_sem=recv_sem.at[origin, which],
            device_id=(x_peer, branch),
            device_id_type=MESH,
        ).wait_recv()

    def y_copy(i):
        source, target = ((q_ref, q_all), (res_ref, r_all))[i]
        return pltpu.make_async_remote_copy(
            src_ref=source.at[:, pl.ds(theirs, half)],
            dst_ref=target.at[branch],
            send_sem=y_send.at[i],
            recv_sem=y_recv.at[i],
            device_id=(me, other),
            device_id_type=MESH,
        )

    def send_own(which):
        to_x(level, which, True).start()

        @pl.when(has_above)
        def _():
            to_above(level, which, True).start()

        @pl.when(has_below)
        def _():
            to_below(level, which, True).start()

        to_c(level, side, which, True).start()

    for which in range(classes):
        send_own(which)
        if which < 2:
            y_copy(which).start()

    align = align_ref[...]
    chosen = lax.broadcasted_iota(jnp.int32, (text_len, text_len), 0) == align
    place[...] = jnp.where(chosen, 1.0, 0.0).astype(jnp.bfloat16)
    edit_ids = ids_ref[1:2, :]
    row = lax.broadcasted_iota(jnp.int32, (16, text_len), 0)
    digits = jnp.where(
        row == 0,
        edit_ids >> 16,
        jnp.where(row == 1, (edit_ids >> 8) & 255, jnp.where(row == 2, edit_ids & 255, 0)),
    )
    digits = rows_by_rows(digits.astype(jnp.float32).astype(jnp.bfloat16), place[...])
    moved_ids = digits[0:1, :] * 65536.0 + digits[1:2, :] * 256.0 + digits[2:3, :]
    same = jnp.where(moved_ids == ids_ref[0:1, :].astype(jnp.float32), 1.0, 0.0)

    for i in range(4):
        text_copy(i).wait()

    def columns(pair):
        return pl.ds(pl.multiple_of(pair * wide, wide), wide)

    def move(pair):
        for i in range(2):
            moved[i, :, columns(pair)] = jnp.dot(
                place[...], text[2 * i + 1, :, columns(pair)], preferred_element_type=jnp.float32
            ).astype(jnp.bfloat16)

    paired = level + 1 - 2 * (level % 2)
    relieved = paired < tall

    def relayed(lev, which):
        return jnp.logical_and(lev == paired, relieved) if which >= groups else False

    def forward_x(lev, which):
        if which < groups:
            to_x(lev, which, False).start()
        else:

            @pl.when(jnp.logical_not(relayed(lev, which)))
            def _():
                to_x(lev, which, False).start()

    def to_paired(which):
        origin = index(level, 1 - side, core)
        peer = index(lax.rem(paired, tall), side, core)
        return kv_copy(kv_all.at[origin, which], origin, which, peer, relay_sem.at[which])

    def pass_on(step, which):
        low, high = level - step, level + step

        @pl.when(low >= 0)
        def _():
            arrived(index(low, side, core), which)

            @pl.when(has_above)
            def _():
                to_above(low, which, False).start()

            forward_x(low, which)
            to_c(low, side, which, False).start()

        @pl.when(high < tall)
        def _():
            arrived(index(high, side, core), which)

            @pl.when(has_below)
            def _():
                to_below(high, which, False).start()

            forward_x(high, which)
            to_c(high, side, which, False).start()

    def across(lev, which):
        arrived(index(lev, 1 - side, core), which)
        if which >= groups and lev is level:

            @pl.when(relieved)
            def _():
                to_paired(which).start()

        to_c(lev, 1 - side, which, False).start()

    def pass_core(step, which):
        low, high = level - step, level + step

        @pl.when(low >= 0)
        def _():
            across(low, which)

        @pl.when(high < tall)
        def _():
            across(high, which)

    def from_core(which):
        @pl.loop(0, 2 * tall)
        def _(i):
            arrived(index(i // 2, i % 2, 1 - core), which)

    def moves(step):
        @pl.loop((step - 1) * pairs // (tall - 1), step * pairs // (tall - 1))
        def _(pair):
            move(pair)

    def head_columns(pair, i):
        return pl.ds(pl.multiple_of(pair * wide + i * HD, HD), HD)

    def joined(value):
        flat = value.astype(jnp.float32).reshape(value.shape[0] * value.shape[1], HD)
        return flat.astype(jnp.bfloat16)

    def weigh(group):
        for i in range(grouped):
            head = group * grouped + i
            at = pl.ds(pl.multiple_of(head * HD, HD), HD)
            scores = rows_by_rows(joined(q_all[:, :, at]), joined(kv_all[:, group, :, i * HD : (i + 1) * HD]))
            peak = jnp.max(scores, axis=1, keepdims=True)
            weights = jnp.exp((scores - peak) * scale)
            total = jnp.sum(weights, axis=1, keepdims=True)
            probs[head] = weights.astype(jnp.bfloat16)
            totals[head] = jnp.broadcast_to(total, (2 * rows, HD))

    def span(which, piece):
        size = (part, wide)[which]
        return pl.multiple_of(piece * size, HD), size

    def back_copy(which, piece):
        source, target = ((att, att_ref), (out, out_ref))[which]
        start, size = span(which, piece)
        return pltpu.make_async_remote_copy(
            src_ref=source.at[other, :, pl.ds(start, size)],
            dst_ref=target.at[:, pl.ds(pl.multiple_of(mine + start, HD), size)],
            send_sem=back_send.at[which, piece],
            recv_sem=back_recv.at[which, piece],
            device_id=(me, other),
            device_id_type=MESH,
        )

    def own_out(which, piece):
        source, target = ((att, att_ref), (out, out_ref))[which]
        start, size = span(which, piece)
        return pltpu.make_async_copy(
            source.at[branch, :, pl.ds(start, size)],
            target.at[:, pl.ds(pl.multiple_of(mine + start, HD), size)],
            own_out_sem.at[which, piece],
        )

    tall_rows = squares.shape[0]
    squares[...] = jnp.zeros((tall_rows, HD), jnp.float32)

    def attend(group):
        added = squares[0 : 2 * rows, :]
        for i in range(grouped):
            head = group * grouped + i
            at = slice(head * HD, (head + 1) * HD)
            values = joined(kv_all[:, groups + group, :, i * HD : (i + 1) * HD])
            summed = jnp.dot(probs[head], values, preferred_element_type=jnp.float32)
            rounded = (summed / totals[head]).reshape(2, rows, HD).astype(jnp.bfloat16)
            att[:, :, at] = rounded
            middle = r_all[:, :, at].astype(jnp.float32) + rounded.astype(jnp.float32)
            mid[:, :, at] = middle
            middle = middle.reshape(2 * rows, HD)
            added = added + middle * middle
        squares[0 : 2 * rows, :] = added
        back_copy(0, group).start()
        own_out(0, group).start()

    @pl.loop(1, tall + classes)
    def _(turn):
        for which in range(classes):
            step = turn - which

            @pl.when(jnp.logical_and(step >= 1, step < tall))
            def _():
                pass_on(step, which)

            @pl.when(step == 1)
            def _():
                across(level, which)

            @pl.when(jnp.logical_and(step >= 2, step <= tall))
            def _():
                pass_core(step - 1, which)

        @pl.when(turn < tall)
        def _():
            moves(turn)

        for which in range(classes - 1):

            @pl.when(turn == tall + which)
            def _():
                if which == 0:
                    own_copy(0).wait()
                    y_copy(0).wait_recv()
                if which == groups:
                    own_copy(1).wait()
                    y_copy(1).wait_recv()
                own_copy(2 + which).wait()
                from_core(which)
                if which < groups:
                    weigh(which)
                else:
                    attend(which - groups)

    if groups == 1:
        own_copy(1).wait()
        y_copy(1).wait_recv()
    own_copy(1 + classes).wait()
    from_core(classes - 1)
    attend(groups - 1)

    lanes = jnp.sum(squares[...].T, axis=0, keepdims=True)
    partial[0] = jnp.broadcast_to(lanes, (8, tall_rows))
    square_copy = pltpu.make_async_remote_copy(
        src_ref=partial.at[0],
        dst_ref=partial.at[1],
        send_sem=y_send.at[2],
        recv_sem=y_recv.at[2],
        device_id=(me, other),
        device_id_type=MESH,
    )
    square_copy.start()
    square_copy.wait_recv()
    norm = lax.rsqrt((partial[0, 0:1] + partial[1, 0:1]) * (1.0 / (2 * half)) + 1e-06)
    squares[...] = jnp.broadcast_to(norm, (HD, tall_rows)).T

    def text_map(query, keys):
        scores = rows_by_rows(query, keys)
        weights = jnp.exp((scores - jnp.max(scores, axis=1, keepdims=True)) * scale)
        return weights / jnp.sum(weights, axis=1, keepdims=True)

    @pl.loop(0, pairs)
    def _(pair):
        for i in range(PAIR):
            at = head_columns(pair, i)
            gain = gain_ref[:, pl.ds(pl.multiple_of(mine + pair * wide + i * HD, HD), HD)]
            middle = mid[:, :, at]
            query = middle.reshape(2 * rows, HD) * squares[0 : 2 * rows, :] * gain.astype(jnp.float32)
            query = query.reshape(2, rows, HD).astype(jnp.bfloat16)
            source_map = text_map(query[0], text[0, :, at])
            edit_map = text_map(query[1], moved[0, :, at])
            injected = jnp.where(same > 0.5, source_map, edit_map)
            source_out = jnp.dot(
                source_map.astype(jnp.bfloat16),
                text[2, :, at],
                preferred_element_type=jnp.float32,
            )
            edit_out = jnp.dot(
                injected.astype(jnp.bfloat16),
                moved[1, :, at],
                preferred_element_type=jnp.float32,
            )
            out[0, :, at] = (middle[0] + source_out).astype(jnp.bfloat16)
            out[1, :, at] = (middle[1] + edit_out).astype(jnp.bfloat16)
        back_copy(1, pair).start()
        own_out(1, pair).start()

    for which in range(2):

        @pl.loop(0, (groups, pairs)[which])
        def _(piece):
            back_copy(which, piece).wait()
            own_out(which, piece).wait()

        y_copy(which).wait_send()

    for which in range(classes):

        @pl.loop(0, tall)
        def _(lev):
            @pl.when(jnp.logical_not(relayed(lev, which)))
            def _():
                to_x(lev, which, False).wait_send()

            to_c(lev, 0, which, False).wait_send()
            to_c(lev, 1, which, False).wait_send()

            @pl.when(jnp.logical_and(has_above, lev <= level))
            def _():
                to_above(lev, which, False).wait_send()

            @pl.when(jnp.logical_and(has_below, lev >= level))
            def _():
                to_below(lev, which, False).wait_send()

        if which >= groups:

            @pl.when(relieved)
            def _():
                to_paired(which).wait_send()

    square_copy.wait_send()


def copy_out(att_in, out_in, att_ref, out_ref):
    att_ref[...] = att_in[...]
    out_ref[...] = out_in[...]


def per_device(n, queries, keys_values, residual_in, cross_gain, text_kv, prompt_ids, word_align):
    rows, width = queries.shape[1:]
    half = keys_values.shape[2]
    heads = half // HD
    pairs = heads // PAIR
    text_len = word_align.shape[0]
    keys = n * rows
    tall = n // 4
    grouped = heads // 2 if heads % 2 == 0 else heads
    classes = 2 * heads // grouped
    tall_rows = pl.cdiv(2 * rows, HD) * HD
    vmem = pl.BlockSpec(memory_space=pltpu.VMEM)
    hbm = pl.BlockSpec(memory_space=pl.ANY)
    shape = jax.ShapeDtypeStruct((rows, width), jnp.bfloat16)
    bf16, f32 = jnp.bfloat16, jnp.float32
    dma = pltpu.SemaphoreType.DMA
    attended, result = pl.pallas_call(
        functools.partial(kernel, n),
        out_shape=(shape, shape),
        in_specs=[hbm, hbm, hbm, vmem, hbm, vmem, vmem],
        out_specs=(hbm, hbm),
        scratch_shapes=[
            pltpu.VMEM((2, rows, half), bf16),
            pltpu.VMEM((2, rows, half), bf16),
            pltpu.VMEM((n, classes, rows, grouped * HD), bf16),
            pltpu.VMEM((4, text_len, half), bf16),
            pltpu.VMEM((2, text_len, half), bf16),
            pltpu.VMEM((text_len, text_len), bf16),
            pltpu.VMEM((heads, 2 * rows, keys), bf16),
            pltpu.VMEM((heads, 2 * rows, HD), f32),
            pltpu.VMEM((2, rows, half), bf16),
            pltpu.VMEM((2, rows, half), f32),
            pltpu.VMEM((tall_rows, HD), f32),
            pltpu.VMEM((2, 8, tall_rows), f32),
            pltpu.VMEM((2, rows, half), bf16),
            dma((4,)),
            dma((2 + classes,)),
            dma((2, pairs)),
            dma((n, classes)),
            dma((tall, classes)),
            dma((tall, classes)),
            dma((tall, classes)),
            dma((2 * tall, classes)),
            dma((classes,)),
            dma((3,)),
            dma((3,)),
            dma((2, pairs)),
            dma((2, pairs)),
        ],
        compiler_params=pltpu.CompilerParams(
            collective_id=0, has_side_effects=True, vmem_limit_bytes=60 * 2**20
        ),
    )(
        queries[0],
        keys_values,
        residual_in[0],
        cross_gain[None],
        text_kv,
        prompt_ids,
        word_align[None],
    )
    attended, result = pl.pallas_call(
        copy_out,
        out_shape=(shape, shape),
        in_specs=[vmem, vmem],
        out_specs=(vmem, vmem),
    )(attended, result)
    return (attended[None], result[None])


def solution(mesh):
    in_specs = (
        P("branch", "seq", None),
        P(None, "seq", "branch"),
        P("branch", "seq", None),
        P(),
        P(),
        P(),
        P(),
    )
    out_specs = (P("branch", "seq", None), P("branch", "seq", None))
    return jax.shard_map(
        functools.partial(per_device, mesh.shape["seq"]),
        mesh=mesh,
        in_specs=in_specs,
        out_specs=out_specs,
        check_vma=False,
    )
```

```python
import functools
import math

import jax
import jax.numpy as jnp
from jax import lax
from jax.experimental import pallas as pl
from jax.experimental.pallas import tpu as pltpu
from jax.sharding import PartitionSpec as P

HD = 128
PAIR = 2
MESH = pl.DeviceIdType.MESH


def rows_by_rows(left, right):
    return lax.dot_general(
        left, right, (((1,), (1,)), ((), ())), preferred_element_type=jnp.float32
    )


def kernel(
    n,
    q_ref,
    kv_ref,
    res_ref,
    gain_ref,
    text_ref,
    ids_ref,
    align_ref,
    att_ref,
    out_ref,
    q_all,
    r_all,
    kv_all,
    text,
    moved,
    place,
    probs,
    totals,
    att,
    mid,
    squares,
    partial,
    gains,
    out,
    text_sem,
    own_sem,
    own_out_sem,
    recv_sem,
    send_up,
    send_down,
    send_x,
    send_c,
    relay_sem,
    y_send,
    y_recv,
    back_send,
    back_recv,
):
    rows = q_ref.shape[0]
    half = kv_ref.shape[2]
    heads = half // HD
    pairs = heads // PAIR
    wide = PAIR * HD
    grouped = heads // 2 if heads % 2 == 0 else heads
    groups = heads // grouped
    part = grouped * HD
    classes = 2 * groups
    text_len = text_ref.shape[2]
    tall = n // 4
    scale = 1.0 / math.sqrt(HD)
    me = lax.axis_index("seq")
    branch = lax.axis_index("branch")
    other = 1 - branch
    core = me % 2
    side = (me // 2) % 2
    level = me // 4
    mine = pl.multiple_of(branch * half, HD)
    theirs = pl.multiple_of(other * half, HD)

    def index(lev, sid, cor):
        return lev * 4 + sid * 2 + cor

    def own_kv(which):
        return kv_ref.at[which // groups, :, pl.ds(which % groups * part, part)]

    x_peer = index(level, 1 - side, core)
    c_peer = index(level, side, 1 - core)

    def text_copy(i):
        return pltpu.make_async_copy(
            text_ref.at[i // 2, i % 2, :, pl.ds(mine, half)], text.at[i], text_sem.at[i]
        )

    for i in range(4):
        text_copy(i).start()

    def own_copy(i):
        if i == 0:
            return pltpu.make_async_copy(
                q_ref.at[:, pl.ds(mine, half)], q_all.at[branch], own_sem.at[0]
            )
        if i == 1:
            return pltpu.make_async_copy(
                res_ref.at[:, pl.ds(mine, half)], r_all.at[branch], own_sem.at[1]
            )
        return pltpu.make_async_copy(own_kv(i - 2), kv_all.at[me, i - 2], own_sem.at[i])

    for i in range(2 + classes):
        own_copy(i).start()

    barrier = pltpu.get_barrier_semaphore()

    def greet(seq, bra):
        pl.semaphore_signal(barrier, inc=1, device_id=(seq, bra), device_id_type=MESH)

    has_above = level + 1 < tall
    has_below = level > 0
    above = index((level + 1) % tall, side, core)
    below = index((level + tall - 1) % tall, side, core)

    @pl.when(has_above)
    def _():
        greet(above, branch)

    @pl.when(has_below)
    def _():
        greet(below, branch)

    greet(x_peer, branch)
    greet(c_peer, branch)
    greet(me, other)
    pl.semaphore_wait(barrier, 3 + has_above.astype(jnp.int32) + has_below.astype(jnp.int32))

    def kv_copy(source, origin, which, peer, sem):
        return pltpu.make_async_remote_copy(
            src_ref=source,
            dst_ref=kv_all.at[origin, which],
            send_sem=sem,
            recv_sem=recv_sem.at[origin, which],
            device_id=(peer, branch),
            device_id_type=MESH,
        )

    def to_above(lev, which):
        origin = index(lev, side, core)
        return kv_copy(kv_all.at[origin, which], origin, which, above, send_up.at[lev, which])

    def to_below(lev, which):
        origin = index(lev, side, core)
        return kv_copy(kv_all.at[origin, which], origin, which, below, send_down.at[lev, which])

    def to_x(lev, which):
        origin = index(lev, side, core)
        return kv_copy(kv_all.at[origin, which], origin, which, x_peer, send_x.at[lev, which])

    def to_c(lev, sid, which):
        origin = index(lev, sid, core)
        return kv_copy(kv_all.at[origin, which], origin, which, c_peer, send_c.at[lev * 2 + sid, which])

    def arrived(origin, which):
        pltpu.make_async_remote_copy(
            src_ref=kv_all.at[origin, which],
            dst_ref=kv_all.at[origin, which],
            send_sem=send_x.at[0, which],
            recv_sem=recv_sem.at[origin, which],
            device_id=(x_peer, branch),
            device_id_type=MESH,
        ).wait_recv()

    def y_copy(i):
        source, target = ((q_ref, q_all), (res_ref, r_all))[i]
        return pltpu.make_async_remote_copy(
            src_ref=source.at[:, pl.ds(theirs, half)],
            dst_ref=target.at[branch],
            send_sem=y_send.at[i],
            recv_sem=y_recv.at[i],
            device_id=(me, other),
            device_id_type=MESH,
        )

    def send_own(which):
        to_x(level, which).start()

        @pl.when(has_above)
        def _():
            to_above(level, which).start()

        @pl.when(has_below)
        def _():
            to_below(level, which).start()

        to_c(level, side, which).start()

    for which in range(classes):
        own_copy(2 + which).wait()
        send_own(which)
        if which < 2:
            y_copy(which).start()

    gains[...] = gain_ref[...].astype(jnp.float32).reshape(1, 2 * half)
    align = align_ref[...]
    chosen = lax.broadcasted_iota(jnp.int32, (text_len, text_len), 0) == align
    place[...] = jnp.where(chosen, 1.0, 0.0).astype(jnp.bfloat16)
    edit_ids = ids_ref[1:2, :]
    row = lax.broadcasted_iota(jnp.int32, (16, text_len), 0)
    digits = jnp.where(
        row == 0,
        edit_ids >> 16,
        jnp.where(row == 1, (edit_ids >> 8) & 255, jnp.where(row == 2, edit_ids & 255, 0)),
    )
    digits = rows_by_rows(digits.astype(jnp.float32).astype(jnp.bfloat16), place[...])
    moved_ids = digits[0:1, :] * 65536.0 + digits[1:2, :] * 256.0 + digits[2:3, :]
    same = jnp.where(moved_ids == ids_ref[0:1, :].astype(jnp.float32), 1.0, 0.0)

    for i in range(4):
        text_copy(i).wait()

    def columns(pair):
        return pl.ds(pl.multiple_of(pair * wide, wide), wide)

    def move(pair):
        for i in range(2):
            moved[i, :, columns(pair)] = jnp.dot(
                place[...], text[2 * i + 1, :, columns(pair)], preferred_element_type=jnp.float32
            ).astype(jnp.bfloat16)

    paired = level + 1 - 2 * (level % 2)
    relieved = paired < tall

    def relayed(lev, which):
        return jnp.logical_and(lev == paired, relieved) if which >= groups else False

    def forward_x(lev, which):
        if which < groups:
            to_x(lev, which).start()
        else:

            @pl.when(jnp.logical_not(relayed(lev, which)))
            def _():
                to_x(lev, which).start()

    def to_paired(which):
        origin = index(level, 1 - side, core)
        peer = index(lax.rem(paired, tall), side, core)
        return kv_copy(kv_all.at[origin, which], origin, which, peer, relay_sem.at[which])

    def pass_on(step, which):
        low, high = level - step, level + step

        @pl.when(low >= 0)
        def _():
            arrived(index(low, side, core), which)

            @pl.when(has_above)
            def _():
                to_above(low, which).start()

            forward_x(low, which)
            to_c(low, side, which).start()

        @pl.when(high < tall)
        def _():
            arrived(index(high, side, core), which)

            @pl.when(has_below)
            def _():
                to_below(high, which).start()

            forward_x(high, which)
            to_c(high, side, which).start()

    def across(lev, which):
        arrived(index(lev, 1 - side, core), which)
        if which >= groups and lev is level:

            @pl.when(relieved)
            def _():
                to_paired(which).start()

        to_c(lev, 1 - side, which).start()

    def pass_core(step, which):
        low, high = level - step, level + step

        @pl.when(low >= 0)
        def _():
            across(low, which)

        @pl.when(high < tall)
        def _():
            across(high, which)

    def from_core(which):
        @pl.loop(0, 2 * tall)
        def _(i):
            arrived(index(i // 2, i % 2, 1 - core), which)

    def moves(step):
        @pl.loop((step - 1) * pairs // (tall - 1), step * pairs // (tall - 1))
        def _(pair):
            move(pair)

    def head_columns(pair, i):
        return pl.ds(pl.multiple_of(pair * wide + i * HD, HD), HD)

    def joined(value):
        flat = value.astype(jnp.float32).reshape(value.shape[0] * value.shape[1], HD)
        return flat.astype(jnp.bfloat16)

    def weigh(group):
        for i in range(grouped):
            head = group * grouped + i
            at = pl.ds(pl.multiple_of(head * HD, HD), HD)
            scores = rows_by_rows(joined(q_all[:, :, at]), joined(kv_all[:, group, :, i * HD : (i + 1) * HD]))
            peak = jnp.max(scores, axis=1, keepdims=True)
            weights = jnp.exp((scores - peak) * scale)
            total = jnp.sum(weights, axis=1, keepdims=True)
            probs[head] = weights.astype(jnp.bfloat16)
            totals[head] = jnp.broadcast_to(total, (2 * rows, HD))

    def span(which, piece):
        size = (part, wide)[which]
        return pl.multiple_of(piece * size, HD), size

    def back_copy(which, piece):
        source, target = ((att, att_ref), (out, out_ref))[which]
        start, size = span(which, piece)
        return pltpu.make_async_remote_copy(
            src_ref=source.at[other, :, pl.ds(start, size)],
            dst_ref=target.at[:, pl.ds(pl.multiple_of(mine + start, HD), size)],
            send_sem=back_send.at[which, piece],
            recv_sem=back_recv.at[which, piece],
            device_id=(me, other),
            device_id_type=MESH,
        )

    def own_out(which, piece):
        source, target = ((att, att_ref), (out, out_ref))[which]
        start, size = span(which, piece)
        return pltpu.make_async_copy(
            source.at[branch, :, pl.ds(start, size)],
            target.at[:, pl.ds(pl.multiple_of(mine + start, HD), size)],
            own_out_sem.at[which, piece],
        )

    tall_rows = squares.shape[0]
    squares[...] = jnp.zeros((tall_rows, HD), jnp.float32)

    def attend(group):
        added = squares[0 : 2 * rows, :]
        for i in range(grouped):
            head = group * grouped + i
            at = slice(head * HD, (head + 1) * HD)
            values = joined(kv_all[:, groups + group, :, i * HD : (i + 1) * HD])
            summed = jnp.dot(probs[head], values, preferred_element_type=jnp.float32)
            rounded = (summed / totals[head]).reshape(2, rows, HD).astype(jnp.bfloat16)
            att[:, :, at] = rounded
            middle = r_all[:, :, at].astype(jnp.float32) + rounded.astype(jnp.float32)
            mid[:, :, at] = middle
            middle = middle.reshape(2 * rows, HD)
            added = added + middle * middle
        squares[0 : 2 * rows, :] = added
        back_copy(0, group).start()
        own_out(0, group).start()

    def compute(which):
        if which == 0:
            own_copy(0).wait()
            y_copy(0).wait_recv()
        if which == groups:
            own_copy(1).wait()
            y_copy(1).wait_recv()
        from_core(which)
        if which < groups:
            weigh(which)
        else:
            attend(which - groups)

    @pl.loop(1, tall - 1)
    def _(step):
        for which in range(classes):
            pass_on(step, which)

            @pl.when(step == 1)
            def _():
                across(level, which)

            @pl.when(step > 1)
            def _():
                pass_core(step - 1, which)

        moves(step)

    moves(tall - 1)
    for which in range(classes):
        pass_on(tall - 1, which)
        if tall == 2:
            across(level, which)
        else:
            pass_core(tall - 2, which)
        if which > 0:
            pass_core(tall - 1, which - 1)
            compute(which - 1)
    pass_core(tall - 1, classes - 1)
    compute(classes - 1)

    lanes = jnp.sum(squares[...].T, axis=0, keepdims=True)
    partial[0] = jnp.broadcast_to(lanes, (8, tall_rows))
    square_copy = pltpu.make_async_remote_copy(
        src_ref=partial.at[0],
        dst_ref=partial.at[1],
        send_sem=y_send.at[2],
        recv_sem=y_recv.at[2],
        device_id=(me, other),
        device_id_type=MESH,
    )
    square_copy.start()
    square_copy.wait_recv()
    norm = lax.rsqrt((partial[0, 0:1] + partial[1, 0:1]) * (1.0 / (2 * half)) + 1e-06)
    squares[...] = jnp.broadcast_to(norm, (HD, tall_rows)).T

    def text_map(query, keys):
        scores = rows_by_rows(query, keys)
        weights = jnp.exp((scores - jnp.max(scores, axis=1, keepdims=True)) * scale)
        return weights / jnp.sum(weights, axis=1, keepdims=True)

    @pl.loop(0, pairs)
    def _(pair):
        for i in range(PAIR):
            at = head_columns(pair, i)
            gain = gains[:, pl.ds(pl.multiple_of(mine + pair * wide + i * HD, HD), HD)]
            middle = mid[:, :, at]
            query = middle.reshape(2 * rows, HD) * squares[0 : 2 * rows, :] * gain
            query = query.reshape(2, rows, HD).astype(jnp.bfloat16)
            source_map = text_map(query[0], text[0, :, at])
            edit_map = text_map(query[1], moved[0, :, at])
            injected = jnp.where(same > 0.5, source_map, edit_map)
            source_out = jnp.dot(
                source_map.astype(jnp.bfloat16),
                text[2, :, at],
                preferred_element_type=jnp.float32,
            )
            edit_out = jnp.dot(
                injected.astype(jnp.bfloat16),
                moved[1, :, at],
                preferred_element_type=jnp.float32,
            )
            out[0, :, at] = (middle[0] + source_out).astype(jnp.bfloat16)
            out[1, :, at] = (middle[1] + edit_out).astype(jnp.bfloat16)
        back_copy(1, pair).start()
        own_out(1, pair).start()

    for which in range(2):

        @pl.loop(0, (groups, pairs)[which])
        def _(piece):
            back_copy(which, piece).wait()
            own_out(which, piece).wait()

        y_copy(which).wait_send()

    for which in range(classes):

        @pl.loop(0, tall)
        def _(lev):
            @pl.when(jnp.logical_not(relayed(lev, which)))
            def _():
                to_x(lev, which).wait_send()

            to_c(lev, 0, which).wait_send()
            to_c(lev, 1, which).wait_send()

            @pl.when(jnp.logical_and(has_above, lev <= level))
            def _():
                to_above(lev, which).wait_send()

            @pl.when(jnp.logical_and(has_below, lev >= level))
            def _():
                to_below(lev, which).wait_send()

        if which >= groups:

            @pl.when(relieved)
            def _():
                to_paired(which).wait_send()

    square_copy.wait_send()


def copy_out(att_in, out_in, att_ref, out_ref):
    att_ref[...] = att_in[...]
    out_ref[...] = out_in[...]


def per_device(n, queries, keys_values, residual_in, cross_gain, text_kv, prompt_ids, word_align):
    rows, width = queries.shape[1:]
    half = keys_values.shape[2]
    heads = half // HD
    pairs = heads // PAIR
    text_len = word_align.shape[0]
    keys = n * rows
    tall = n // 4
    grouped = heads // 2 if heads % 2 == 0 else heads
    classes = 2 * heads // grouped
    tall_rows = pl.cdiv(2 * rows, HD) * HD
    vmem = pl.BlockSpec(memory_space=pltpu.VMEM)
    hbm = pl.BlockSpec(memory_space=pl.ANY)
    shape = jax.ShapeDtypeStruct((rows, width), jnp.bfloat16)
    bf16, f32 = jnp.bfloat16, jnp.float32
    dma = pltpu.SemaphoreType.DMA
    attended, result = pl.pallas_call(
        functools.partial(kernel, n),
        out_shape=(shape, shape),
        in_specs=[hbm, hbm, hbm, vmem, hbm, vmem, vmem],
        out_specs=(hbm, hbm),
        scratch_shapes=[
            pltpu.VMEM((2, rows, half), bf16),
            pltpu.VMEM((2, rows, half), bf16),
            pltpu.VMEM((n, classes, rows, grouped * HD), bf16),
            pltpu.VMEM((4, text_len, half), bf16),
            pltpu.VMEM((2, text_len, half), bf16),
            pltpu.VMEM((text_len, text_len), bf16),
            pltpu.VMEM((heads, 2 * rows, keys), bf16),
            pltpu.VMEM((heads, 2 * rows, HD), f32),
            pltpu.VMEM((2, rows, half), bf16),
            pltpu.VMEM((2, rows, half), f32),
            pltpu.VMEM((tall_rows, HD), f32),
            pltpu.VMEM((2, 8, tall_rows), f32),
            pltpu.VMEM((1, width), f32),
            pltpu.VMEM((2, rows, half), bf16),
            dma((4,)),
            dma((2 + classes,)),
            dma((2, pairs)),
            dma((n, classes)),
            dma((tall, classes)),
            dma((tall, classes)),
            dma((tall, classes)),
            dma((2 * tall, classes)),
            dma((classes,)),
            dma((3,)),
            dma((3,)),
            dma((2, pairs)),
            dma((2, pairs)),
        ],
        compiler_params=pltpu.CompilerParams(
            collective_id=0, has_side_effects=True, vmem_limit_bytes=60 * 2**20
        ),
    )(
        queries[0],
        keys_values,
        residual_in[0],
        cross_gain,
        text_kv,
        prompt_ids,
        word_align[None],
    )
    attended, result = pl.pallas_call(
        copy_out,
        out_shape=(shape, shape),
        in_specs=[vmem, vmem],
        out_specs=(vmem, vmem),
    )(attended, result)
    return (attended[None], result[None])


def solution(mesh):
    in_specs = (
        P("branch", "seq", None),
        P(None, "seq", "branch"),
        P("branch", "seq", None),
        P(),
        P(),
        P(),
        P(),
    )
    out_specs = (P("branch", "seq", None), P("branch", "seq", None))
    return jax.shard_map(
        functools.partial(per_device, mesh.shape["seq"]),
        mesh=mesh,
        in_specs=in_specs,
        out_specs=out_specs,
        check_vma=False,
    )
```

```python
import functools
import math

import jax
import jax.numpy as jnp
from jax import lax
from jax.experimental import pallas as pl
from jax.experimental.pallas import tpu as pltpu
from jax.sharding import PartitionSpec as P

HD = 128
PAIR = 2
MESH = pl.DeviceIdType.MESH


def rows_by_rows(left, right):
    return lax.dot_general(
        left, right, (((1,), (1,)), ((), ())), preferred_element_type=jnp.float32
    )


def kernel(
    n,
    q_ref,
    kv_ref,
    res_ref,
    gain_ref,
    text_ref,
    ids_ref,
    align_ref,
    att_ref,
    out_ref,
    q_all,
    r_all,
    kv_all,
    text,
    moved,
    place,
    probs,
    totals,
    att,
    mid,
    squares,
    partial,
    gains,
    out,
    text_sem,
    own_sem,
    own_out_sem,
    recv_sem,
    send_up,
    send_down,
    send_x,
    send_c,
    relay_sem,
    y_send,
    y_recv,
    back_send,
    back_recv,
):
    rows = q_ref.shape[0]
    half = kv_ref.shape[2]
    heads = half // HD
    pairs = heads // PAIR
    wide = PAIR * HD
    grouped = heads // 2 if heads % 2 == 0 else heads
    groups = heads // grouped
    part = grouped * HD
    classes = 2 * groups
    text_len = text_ref.shape[2]
    tall = n // 4
    scale = 1.0 / math.sqrt(HD)
    me = lax.axis_index("seq")
    branch = lax.axis_index("branch")
    other = 1 - branch
    core = me % 2
    side = (me // 2) % 2
    level = me // 4
    mine = pl.multiple_of(branch * half, HD)
    theirs = pl.multiple_of(other * half, HD)

    def index(lev, sid, cor):
        return lev * 4 + sid * 2 + cor

    def own_kv(which):
        return kv_ref.at[which // groups, :, pl.ds(which % groups * part, part)]

    x_peer = index(level, 1 - side, core)
    c_peer = index(level, side, 1 - core)

    def text_copy(i):
        return pltpu.make_async_copy(
            text_ref.at[i // 2, i % 2, :, pl.ds(mine, half)], text.at[i], text_sem.at[i]
        )

    def own_copy(i):
        if i == 0:
            return pltpu.make_async_copy(
                q_ref.at[:, pl.ds(mine, half)], q_all.at[branch], own_sem.at[0]
            )
        if i == 1:
            return pltpu.make_async_copy(
                res_ref.at[:, pl.ds(mine, half)], r_all.at[branch], own_sem.at[1]
            )
        return pltpu.make_async_copy(own_kv(i - 2), kv_all.at[me, i - 2], own_sem.at[i])

    for i in (*range(2, 2 + classes), 0, 1):
        own_copy(i).start()
    for i in (1, 3, 0, 2):
        text_copy(i).start()

    barrier = pltpu.get_barrier_semaphore()

    def greet(seq, bra):
        pl.semaphore_signal(barrier, inc=1, device_id=(seq, bra), device_id_type=MESH)

    has_above = level + 1 < tall
    has_below = level > 0
    above = index((level + 1) % tall, side, core)
    below = index((level + tall - 1) % tall, side, core)

    @pl.when(has_above)
    def _():
        greet(above, branch)

    @pl.when(has_below)
    def _():
        greet(below, branch)

    greet(x_peer, branch)
    greet(c_peer, branch)
    greet(me, other)
    pl.semaphore_wait(barrier, 3 + has_above.astype(jnp.int32) + has_below.astype(jnp.int32))

    def kv_copy(source, origin, which, peer, sem):
        return pltpu.make_async_remote_copy(
            src_ref=source,
            dst_ref=kv_all.at[origin, which],
            send_sem=sem,
            recv_sem=recv_sem.at[origin, which],
            device_id=(peer, branch),
            device_id_type=MESH,
        )

    def to_above(lev, which):
        origin = index(lev, side, core)
        return kv_copy(kv_all.at[origin, which], origin, which, above, send_up.at[lev, which])

    def to_below(lev, which):
        origin = index(lev, side, core)
        return kv_copy(kv_all.at[origin, which], origin, which, below, send_down.at[lev, which])

    def to_x(lev, which):
        origin = index(lev, side, core)
        return kv_copy(kv_all.at[origin, which], origin, which, x_peer, send_x.at[lev, which])

    def to_c(lev, sid, which):
        origin = index(lev, sid, core)
        return kv_copy(kv_all.at[origin, which], origin, which, c_peer, send_c.at[lev * 2 + sid, which])

    def arrived(origin, which):
        pltpu.make_async_remote_copy(
            src_ref=kv_all.at[origin, which],
            dst_ref=kv_all.at[origin, which],
            send_sem=send_x.at[0, which],
            recv_sem=recv_sem.at[origin, which],
            device_id=(x_peer, branch),
            device_id_type=MESH,
        ).wait_recv()

    def y_copy(i):
        source, target = ((q_ref, q_all), (res_ref, r_all))[i]
        return pltpu.make_async_remote_copy(
            src_ref=source.at[:, pl.ds(theirs, half)],
            dst_ref=target.at[branch],
            send_sem=y_send.at[i],
            recv_sem=y_recv.at[i],
            device_id=(me, other),
            device_id_type=MESH,
        )

    def send_own(which):
        to_x(level, which).start()

        @pl.when(has_above)
        def _():
            to_above(level, which).start()

        @pl.when(has_below)
        def _():
            to_below(level, which).start()

        to_c(level, side, which).start()

    for which in range(classes):
        own_copy(2 + which).wait()
        send_own(which)
        if which < 2:
            y_copy(which).start()

    gains[...] = gain_ref[...].astype(jnp.float32).reshape(1, 2 * half)
    align = align_ref[...]
    chosen = lax.broadcasted_iota(jnp.int32, (text_len, text_len), 0) == align
    place[...] = jnp.where(chosen, 1.0, 0.0).astype(jnp.bfloat16)
    edit_ids = ids_ref[1:2, :]
    row = lax.broadcasted_iota(jnp.int32, (16, text_len), 0)
    digits = jnp.where(
        row == 0,
        edit_ids >> 16,
        jnp.where(row == 1, (edit_ids >> 8) & 255, jnp.where(row == 2, edit_ids & 255, 0)),
    )
    digits = rows_by_rows(digits.astype(jnp.float32).astype(jnp.bfloat16), place[...])
    moved_ids = digits[0:1, :] * 65536.0 + digits[1:2, :] * 256.0 + digits[2:3, :]
    same = jnp.where(moved_ids == ids_ref[0:1, :].astype(jnp.float32), 1.0, 0.0)

    for i in range(4):
        text_copy(i).wait()

    def columns(pair):
        return pl.ds(pl.multiple_of(pair * wide, wide), wide)

    def move(pair):
        for i in range(2):
            moved[i, :, columns(pair)] = jnp.dot(
                place[...], text[2 * i + 1, :, columns(pair)], preferred_element_type=jnp.float32
            ).astype(jnp.bfloat16)

    paired = level + 1 - 2 * (level % 2)
    relieved = paired < tall

    def relayed(lev, which):
        return jnp.logical_and(lev == paired, relieved) if which >= groups else False

    def forward_x(lev, which):
        if which < groups:
            to_x(lev, which).start()
        else:

            @pl.when(jnp.logical_not(relayed(lev, which)))
            def _():
                to_x(lev, which).start()

    def to_paired(which):
        origin = index(level, 1 - side, core)
        peer = index(lax.rem(paired, tall), side, core)
        return kv_copy(kv_all.at[origin, which], origin, which, peer, relay_sem.at[which])

    def pass_on(step, which):
        low, high = level - step, level + step

        @pl.when(low >= 0)
        def _():
            arrived(index(low, side, core), which)

            @pl.when(has_above)
            def _():
                to_above(low, which).start()

            forward_x(low, which)
            to_c(low, side, which).start()

        @pl.when(high < tall)
        def _():
            arrived(index(high, side, core), which)

            @pl.when(has_below)
            def _():
                to_below(high, which).start()

            forward_x(high, which)
            to_c(high, side, which).start()

    def across(lev, which):
        arrived(index(lev, 1 - side, core), which)
        if which >= groups and lev is level:

            @pl.when(relieved)
            def _():
                to_paired(which).start()

        to_c(lev, 1 - side, which).start()

    def pass_core(step, which):
        low, high = level - step, level + step

        @pl.when(low >= 0)
        def _():
            across(low, which)

        @pl.when(high < tall)
        def _():
            across(high, which)

    def from_core(which):
        @pl.loop(0, 2 * tall)
        def _(i):
            arrived(index(i // 2, i % 2, 1 - core), which)

    def moves(step):
        @pl.loop((step - 1) * pairs // (tall - 1), step * pairs // (tall - 1))
        def _(pair):
            move(pair)

    def head_columns(pair, i):
        return pl.ds(pl.multiple_of(pair * wide + i * HD, HD), HD)

    def joined(value):
        flat = value.astype(jnp.float32).reshape(value.shape[0] * value.shape[1], HD)
        return flat.astype(jnp.bfloat16)

    def weigh(group):
        for i in range(grouped):
            head = group * grouped + i
            at = pl.ds(pl.multiple_of(head * HD, HD), HD)
            scores = rows_by_rows(joined(q_all[:, :, at]), joined(kv_all[:, group, :, i * HD : (i + 1) * HD]))
            peak = jnp.max(scores, axis=1, keepdims=True)
            weights = jnp.exp((scores - peak) * scale)
            total = jnp.sum(weights, axis=1, keepdims=True)
            probs[head] = weights.astype(jnp.bfloat16)
            totals[head] = jnp.broadcast_to(1.0 / total, (2 * rows, HD))

    def span(which, piece):
        size = (part, wide)[which]
        return pl.multiple_of(piece * size, HD), size

    def back_copy(which, piece):
        source, target = ((att, att_ref), (out, out_ref))[which]
        start, size = span(which, piece)
        return pltpu.make_async_remote_copy(
            src_ref=source.at[other, :, pl.ds(start, size)],
            dst_ref=target.at[:, pl.ds(pl.multiple_of(mine + start, HD), size)],
            send_sem=back_send.at[which, piece],
            recv_sem=back_recv.at[which, piece],
            device_id=(me, other),
            device_id_type=MESH,
        )

    def own_out(which, piece):
        source, target = ((att, att_ref), (out, out_ref))[which]
        start, size = span(which, piece)
        return pltpu.make_async_copy(
            source.at[branch, :, pl.ds(start, size)],
            target.at[:, pl.ds(pl.multiple_of(mine + start, HD), size)],
            own_out_sem.at[which, piece],
        )

    tall_rows = squares.shape[0]
    squares[...] = jnp.zeros((tall_rows, HD), jnp.float32)

    def attend(group):
        added = squares[0 : 2 * rows, :]
        for i in range(grouped):
            head = group * grouped + i
            at = slice(head * HD, (head + 1) * HD)
            values = joined(kv_all[:, groups + group, :, i * HD : (i + 1) * HD])
            summed = jnp.dot(probs[head], values, preferred_element_type=jnp.float32)
            rounded = (summed * totals[head]).reshape(2, rows, HD).astype(jnp.bfloat16)
            att[:, :, at] = rounded
            middle = r_all[:, :, at].astype(jnp.float32) + rounded.astype(jnp.float32)
            mid[:, :, at] = middle
            middle = middle.reshape(2 * rows, HD)
            added = added + middle * middle
        squares[0 : 2 * rows, :] = added
        back_copy(0, group).start()
        own_out(0, group).start()

    def compute(which):
        if which == 0:
            own_copy(0).wait()
            y_copy(0).wait_recv()
        if which == groups:
            own_copy(1).wait()
            y_copy(1).wait_recv()
        from_core(which)
        if which < groups:
            weigh(which)
        else:
            attend(which - groups)

    @pl.loop(1, tall - 1)
    def _(step):
        for which in range(classes):
            pass_on(step, which)

            @pl.when(step == 1)
            def _():
                across(level, which)

            @pl.when(step > 1)
            def _():
                pass_core(step - 1, which)

        moves(step)

    moves(tall - 1)
    for which in range(classes):
        pass_on(tall - 1, which)
        if tall == 2:
            across(level, which)
        else:
            pass_core(tall - 2, which)
        if which > 0:
            pass_core(tall - 1, which - 1)
            compute(which - 1)
    pass_core(tall - 1, classes - 1)
    compute(classes - 1)

    lanes = jnp.sum(squares[...].T, axis=0, keepdims=True)
    partial[0] = jnp.broadcast_to(lanes, (8, tall_rows))
    square_copy = pltpu.make_async_remote_copy(
        src_ref=partial.at[0],
        dst_ref=partial.at[1],
        send_sem=y_send.at[2],
        recv_sem=y_recv.at[2],
        device_id=(me, other),
        device_id_type=MESH,
    )
    square_copy.start()
    square_copy.wait_recv()
    norm = lax.rsqrt((partial[0, 0:1] + partial[1, 0:1]) * (1.0 / (2 * half)) + 1e-06)
    squares[...] = jnp.broadcast_to(norm, (HD, tall_rows)).T

    def text_map(query, keys):
        scores = rows_by_rows(query, keys)
        weights = jnp.exp((scores - jnp.max(scores, axis=1, keepdims=True)) * scale)
        return weights * (1.0 / jnp.sum(weights, axis=1, keepdims=True))

    @pl.loop(0, pairs)
    def _(pair):
        for i in range(PAIR):
            at = head_columns(pair, i)
            gain = gains[:, pl.ds(pl.multiple_of(mine + pair * wide + i * HD, HD), HD)]
            middle = mid[:, :, at]
            query = middle.reshape(2 * rows, HD) * squares[0 : 2 * rows, :] * gain
            query = query.reshape(2, rows, HD).astype(jnp.bfloat16)
            source_map = text_map(query[0], text[0, :, at])
            edit_map = text_map(query[1], moved[0, :, at])
            injected = jnp.where(same > 0.5, source_map, edit_map)
            source_out = jnp.dot(
                source_map.astype(jnp.bfloat16),
                text[2, :, at],
                preferred_element_type=jnp.float32,
            )
            edit_out = jnp.dot(
                injected.astype(jnp.bfloat16),
                moved[1, :, at],
                preferred_element_type=jnp.float32,
            )
            out[0, :, at] = (middle[0] + source_out).astype(jnp.bfloat16)
            out[1, :, at] = (middle[1] + edit_out).astype(jnp.bfloat16)
        back_copy(1, pair).start()
        own_out(1, pair).start()

    for which in range(2):

        @pl.loop(0, (groups, pairs)[which])
        def _(piece):
            back_copy(which, piece).wait()
            own_out(which, piece).wait()

        y_copy(which).wait_send()

    for which in range(classes):

        @pl.loop(0, tall)
        def _(lev):
            @pl.when(jnp.logical_not(relayed(lev, which)))
            def _():
                to_x(lev, which).wait_send()

            to_c(lev, 0, which).wait_send()
            to_c(lev, 1, which).wait_send()

            @pl.when(jnp.logical_and(has_above, lev <= level))
            def _():
                to_above(lev, which).wait_send()

            @pl.when(jnp.logical_and(has_below, lev >= level))
            def _():
                to_below(lev, which).wait_send()

        if which >= groups:

            @pl.when(relieved)
            def _():
                to_paired(which).wait_send()

    square_copy.wait_send()


def copy_out(att_in, out_in, att_ref, out_ref, sem):
    copies = (
        pltpu.make_async_copy(att_in, att_ref, sem.at[0]),
        pltpu.make_async_copy(out_in, out_ref, sem.at[1]),
    )
    for copy in copies:
        copy.start()
    for copy in copies:
        copy.wait()


def per_device(n, queries, keys_values, residual_in, cross_gain, text_kv, prompt_ids, word_align):
    rows, width = queries.shape[1:]
    half = keys_values.shape[2]
    heads = half // HD
    pairs = heads // PAIR
    text_len = word_align.shape[0]
    keys = n * rows
    tall = n // 4
    grouped = heads // 2 if heads % 2 == 0 else heads
    classes = 2 * heads // grouped
    tall_rows = pl.cdiv(2 * rows, HD) * HD
    vmem = pl.BlockSpec(memory_space=pltpu.VMEM)
    hbm = pl.BlockSpec(memory_space=pl.ANY)
    shape = jax.ShapeDtypeStruct((rows, width), jnp.bfloat16)
    bf16, f32 = jnp.bfloat16, jnp.float32
    dma = pltpu.SemaphoreType.DMA
    attended, result = pl.pallas_call(
        functools.partial(kernel, n),
        out_shape=(pltpu.VMEM((rows, width), bf16), pltpu.VMEM((rows, width), bf16)),
        in_specs=[hbm, hbm, hbm, vmem, hbm, vmem, vmem],
        out_specs=(vmem, vmem),
        scratch_shapes=[
            pltpu.VMEM((2, rows, half), bf16),
            pltpu.VMEM((2, rows, half), bf16),
            pltpu.VMEM((n, classes, rows, grouped * HD), bf16),
            pltpu.VMEM((4, text_len, half), bf16),
            pltpu.VMEM((2, text_len, half), bf16),
            pltpu.VMEM((text_len, text_len), bf16),
            pltpu.VMEM((heads, 2 * rows, keys), bf16),
            pltpu.VMEM((heads, 2 * rows, HD), f32),
            pltpu.VMEM((2, rows, half), bf16),
            pltpu.VMEM((2, rows, half), f32),
            pltpu.VMEM((tall_rows, HD), f32),
            pltpu.VMEM((2, 8, tall_rows), f32),
            pltpu.VMEM((1, width), f32),
            pltpu.VMEM((2, rows, half), bf16),
            dma((4,)),
            dma((2 + classes,)),
            dma((2, pairs)),
            dma((n, classes)),
            dma((tall, classes)),
            dma((tall, classes)),
            dma((tall, classes)),
            dma((2 * tall, classes)),
            dma((classes,)),
            dma((3,)),
            dma((3,)),
            dma((2, pairs)),
            dma((2, pairs)),
        ],
        compiler_params=pltpu.CompilerParams(
            collective_id=0, has_side_effects=True, vmem_limit_bytes=60 * 2**20
        ),
    )(
        queries[0],
        keys_values,
        residual_in[0],
        cross_gain,
        text_kv,
        prompt_ids,
        word_align[None],
    )
    attended, result = pl.pallas_call(
        copy_out,
        out_shape=(shape, shape),
        in_specs=[vmem, vmem],
        out_specs=(hbm, hbm),
        scratch_shapes=[dma((2,))],
    )(attended, result)
    return (attended[None], result[None])


def solution(mesh):
    in_specs = (
        P("branch", "seq", None),
        P(None, "seq", "branch"),
        P("branch", "seq", None),
        P(),
        P(),
        P(),
        P(),
    )
    out_specs = (P("branch", "seq", None), P("branch", "seq", None))
    return jax.shard_map(
        functools.partial(per_device, mesh.shape["seq"]),
        mesh=mesh,
        in_specs=in_specs,
        out_specs=out_specs,
        check_vma=False,
    )
```

```python
import functools
import math

import jax
import jax.numpy as jnp
from jax import lax
from jax.experimental import pallas as pl
from jax.experimental.pallas import tpu as pltpu
from jax.sharding import PartitionSpec as P

HD = 128
PAIR = 2
CHUNK = 4
MESH = pl.DeviceIdType.MESH


def rows_by_rows(left, right):
    return lax.dot_general(
        left, right, (((1,), (1,)), ((), ())), preferred_element_type=jnp.float32
    )


def kernel(
    n,
    q_ref,
    kv_ref,
    res_ref,
    gain_ref,
    text_ref,
    ids_ref,
    align_ref,
    att_ref,
    out_ref,
    q_all,
    r_all,
    kv_all,
    text,
    moved,
    place,
    probs,
    totals,
    att,
    mid,
    squares,
    partial,
    gains,
    out,
    text_sem,
    own_sem,
    own_out_sem,
    recv_sem,
    send_up,
    send_down,
    send_x,
    send_c,
    relay_sem,
    y_send,
    y_recv,
    back_send,
    back_recv,
):
    rows = q_ref.shape[0]
    half = kv_ref.shape[2]
    heads = half // HD
    pairs = heads // PAIR
    wide = PAIR * HD
    grouped = heads // 2 if heads % 2 == 0 else heads
    groups = heads // grouped
    part = grouped * HD
    classes = 2 * groups
    chunks = pl.cdiv(heads, CHUNK)
    text_len = text_ref.shape[2]
    tall = n // 4
    scale = 1.0 / math.sqrt(HD)
    me = lax.axis_index("seq")
    branch = lax.axis_index("branch")
    other = 1 - branch
    core = me % 2
    side = (me // 2) % 2
    level = me // 4
    mine = pl.multiple_of(branch * half, HD)
    theirs = pl.multiple_of(other * half, HD)

    def index(lev, sid, cor):
        return lev * 4 + sid * 2 + cor

    def own_kv(which):
        return kv_ref.at[which // groups, :, pl.ds(which % groups * part, part)]

    x_peer = index(level, 1 - side, core)
    c_peer = index(level, side, 1 - core)

    def text_copy(i):
        return pltpu.make_async_copy(
            text_ref.at[i // 2, i % 2, :, pl.ds(mine, half)], text.at[i], text_sem.at[i]
        )

    def own_copy(i):
        if i == 0:
            return pltpu.make_async_copy(
                q_ref.at[:, pl.ds(mine, half)], q_all.at[branch], own_sem.at[0]
            )
        if i == 1:
            return pltpu.make_async_copy(
                res_ref.at[:, pl.ds(mine, half)], r_all.at[branch], own_sem.at[1]
            )
        return pltpu.make_async_copy(own_kv(i - 2), kv_all.at[me, i - 2], own_sem.at[i])

    for i in (*range(2, 2 + classes), 0, 1):
        own_copy(i).start()
    for i in (1, 3, 0, 2):
        text_copy(i).start()

    barrier = pltpu.get_barrier_semaphore()

    def greet(seq, bra):
        pl.semaphore_signal(barrier, inc=1, device_id=(seq, bra), device_id_type=MESH)

    has_above = level + 1 < tall
    has_below = level > 0
    above = index((level + 1) % tall, side, core)
    below = index((level + tall - 1) % tall, side, core)

    @pl.when(has_above)
    def _():
        greet(above, branch)

    @pl.when(has_below)
    def _():
        greet(below, branch)

    greet(x_peer, branch)
    greet(c_peer, branch)
    greet(me, other)
    pl.semaphore_wait(barrier, 3 + has_above.astype(jnp.int32) + has_below.astype(jnp.int32))

    def kv_copy(source, origin, which, peer, sem):
        return pltpu.make_async_remote_copy(
            src_ref=source,
            dst_ref=kv_all.at[origin, which],
            send_sem=sem,
            recv_sem=recv_sem.at[origin, which],
            device_id=(peer, branch),
            device_id_type=MESH,
        )

    def to_above(lev, which):
        origin = index(lev, side, core)
        return kv_copy(kv_all.at[origin, which], origin, which, above, send_up.at[lev, which])

    def to_below(lev, which):
        origin = index(lev, side, core)
        return kv_copy(kv_all.at[origin, which], origin, which, below, send_down.at[lev, which])

    def to_x(lev, which):
        origin = index(lev, side, core)
        return kv_copy(kv_all.at[origin, which], origin, which, x_peer, send_x.at[lev, which])

    def to_c(lev, sid, which):
        origin = index(lev, sid, core)
        return kv_copy(kv_all.at[origin, which], origin, which, c_peer, send_c.at[lev * 2 + sid, which])

    def arrived(origin, which):
        pltpu.make_async_remote_copy(
            src_ref=kv_all.at[origin, which],
            dst_ref=kv_all.at[origin, which],
            send_sem=send_x.at[0, which],
            recv_sem=recv_sem.at[origin, which],
            device_id=(x_peer, branch),
            device_id_type=MESH,
        ).wait_recv()

    def y_copy(i):
        source, target = ((q_ref, q_all), (res_ref, r_all))[i]
        return pltpu.make_async_remote_copy(
            src_ref=source.at[:, pl.ds(theirs, half)],
            dst_ref=target.at[branch],
            send_sem=y_send.at[i],
            recv_sem=y_recv.at[i],
            device_id=(me, other),
            device_id_type=MESH,
        )

    def send_own(which):
        to_x(level, which).start()

        @pl.when(has_above)
        def _():
            to_above(level, which).start()

        @pl.when(has_below)
        def _():
            to_below(level, which).start()

        to_c(level, side, which).start()

    for which in range(classes):
        own_copy(2 + which).wait()
        send_own(which)
        if which < 2:
            y_copy(which).start()

    gains[...] = gain_ref[...].astype(jnp.float32).reshape(1, 2 * half)
    align = align_ref[...]
    chosen = lax.broadcasted_iota(jnp.int32, (text_len, text_len), 0) == align
    place[...] = jnp.where(chosen, 1.0, 0.0).astype(jnp.bfloat16)
    edit_ids = ids_ref[1:2, :]
    row = lax.broadcasted_iota(jnp.int32, (16, text_len), 0)
    digits = jnp.where(
        row == 0,
        edit_ids >> 16,
        jnp.where(row == 1, (edit_ids >> 8) & 255, jnp.where(row == 2, edit_ids & 255, 0)),
    )
    digits = rows_by_rows(digits.astype(jnp.float32).astype(jnp.bfloat16), place[...])
    moved_ids = digits[0:1, :] * 65536.0 + digits[1:2, :] * 256.0 + digits[2:3, :]
    same = jnp.where(moved_ids == ids_ref[0:1, :].astype(jnp.float32), 1.0, 0.0)

    for i in range(4):
        text_copy(i).wait()

    def columns(pair):
        return pl.ds(pl.multiple_of(pair * wide, wide), wide)

    def move(pair):
        for i in range(2):
            moved[i, :, columns(pair)] = jnp.dot(
                place[...], text[2 * i + 1, :, columns(pair)], preferred_element_type=jnp.float32
            ).astype(jnp.bfloat16)

    paired = level + 1 - 2 * (level % 2)
    relieved = paired < tall

    def relayed(lev, which):
        return jnp.logical_and(lev == paired, relieved) if which >= groups else False

    def forward_x(lev, which):
        if which < groups:
            to_x(lev, which).start()
        else:

            @pl.when(jnp.logical_not(relayed(lev, which)))
            def _():
                to_x(lev, which).start()

    def to_paired(which):
        origin = index(level, 1 - side, core)
        peer = index(lax.rem(paired, tall), side, core)
        return kv_copy(kv_all.at[origin, which], origin, which, peer, relay_sem.at[which])

    def pass_on(step, which):
        low, high = level - step, level + step

        @pl.when(low >= 0)
        def _():
            arrived(index(low, side, core), which)

            @pl.when(has_above)
            def _():
                to_above(low, which).start()

            forward_x(low, which)
            to_c(low, side, which).start()

        @pl.when(high < tall)
        def _():
            arrived(index(high, side, core), which)

            @pl.when(has_below)
            def _():
                to_below(high, which).start()

            forward_x(high, which)
            to_c(high, side, which).start()

    def across(lev, which):
        arrived(index(lev, 1 - side, core), which)
        if which >= groups and lev is level:

            @pl.when(relieved)
            def _():
                to_paired(which).start()

        to_c(lev, 1 - side, which).start()

    def pass_core(step, which):
        low, high = level - step, level + step

        @pl.when(low >= 0)
        def _():
            across(low, which)

        @pl.when(high < tall)
        def _():
            across(high, which)

    def from_core(which):
        @pl.loop(0, 2 * tall)
        def _(i):
            arrived(index(i // 2, i % 2, 1 - core), which)

    def moves(step):
        @pl.loop((step - 1) * pairs // (tall - 1), step * pairs // (tall - 1))
        def _(pair):
            move(pair)

    def joined(value):
        flat = value.astype(jnp.float32).reshape(value.shape[0] * value.shape[1], HD)
        return flat.astype(jnp.bfloat16)

    def weigh(group):
        for i in range(grouped):
            head = group * grouped + i
            at = pl.ds(pl.multiple_of(head * HD, HD), HD)
            scores = rows_by_rows(joined(q_all[:, :, at]), joined(kv_all[:, group, :, i * HD : (i + 1) * HD]))
            peak = jnp.max(scores, axis=1, keepdims=True)
            weights = jnp.exp((scores - peak) * scale)
            total = jnp.sum(weights, axis=1, keepdims=True)
            probs[head] = weights.astype(jnp.bfloat16)
            totals[head] = jnp.broadcast_to(1.0 / total, (2 * rows, HD))

    def span(which, piece):
        if which == 0:
            return piece * part, part
        return piece * CHUNK * HD, min(CHUNK, heads - piece * CHUNK) * HD

    def back_copy(which, piece):
        source, target = ((att, att_ref), (out, out_ref))[which]
        start, size = span(which, piece)
        return pltpu.make_async_remote_copy(
            src_ref=source.at[other, :, pl.ds(start, size)],
            dst_ref=target.at[:, pl.ds(pl.multiple_of(mine + start, HD), size)],
            send_sem=back_send.at[which, piece],
            recv_sem=back_recv.at[which, piece],
            device_id=(me, other),
            device_id_type=MESH,
        )

    def own_out(which, piece):
        source, target = ((att, att_ref), (out, out_ref))[which]
        start, size = span(which, piece)
        return pltpu.make_async_copy(
            source.at[branch, :, pl.ds(start, size)],
            target.at[:, pl.ds(pl.multiple_of(mine + start, HD), size)],
            own_out_sem.at[which, piece],
        )

    tall_rows = squares.shape[0]
    squares[...] = jnp.zeros((tall_rows, HD), jnp.float32)

    def attend(group):
        added = squares[0 : 2 * rows, :]
        for i in range(grouped):
            head = group * grouped + i
            at = slice(head * HD, (head + 1) * HD)
            values = joined(kv_all[:, groups + group, :, i * HD : (i + 1) * HD])
            summed = jnp.dot(probs[head], values, preferred_element_type=jnp.float32)
            rounded = (summed * totals[head]).reshape(2, rows, HD).astype(jnp.bfloat16)
            att[:, :, at] = rounded
            middle = r_all[:, :, at].astype(jnp.float32) + rounded.astype(jnp.float32)
            mid[:, :, at] = middle
            middle = middle.reshape(2 * rows, HD)
            added = added + middle * middle
        squares[0 : 2 * rows, :] = added
        back_copy(0, group).start()
        own_out(0, group).start()

    def compute(which):
        if which == 0:
            own_copy(0).wait()
            y_copy(0).wait_recv()
        if which == groups:
            own_copy(1).wait()
            y_copy(1).wait_recv()
        from_core(which)
        if which < groups:
            weigh(which)
        else:
            attend(which - groups)

    @pl.loop(1, tall - 1)
    def _(step):
        for which in range(classes):
            pass_on(step, which)

            @pl.when(step == 1)
            def _():
                across(level, which)

            @pl.when(step > 1)
            def _():
                pass_core(step - 1, which)

        moves(step)

    moves(tall - 1)
    for which in range(classes):
        pass_on(tall - 1, which)
        if tall == 2:
            across(level, which)
        else:
            pass_core(tall - 2, which)
        if which > 0:
            pass_core(tall - 1, which - 1)
            compute(which - 1)
    pass_core(tall - 1, classes - 1)
    compute(classes - 1)

    lanes = jnp.sum(squares[...].T, axis=0, keepdims=True)
    partial[0] = jnp.broadcast_to(lanes, (8, tall_rows))
    square_copy = pltpu.make_async_remote_copy(
        src_ref=partial.at[0],
        dst_ref=partial.at[1],
        send_sem=y_send.at[2],
        recv_sem=y_recv.at[2],
        device_id=(me, other),
        device_id_type=MESH,
    )
    square_copy.start()
    square_copy.wait_recv()
    norm = lax.rsqrt((partial[0, 0:1] + partial[1, 0:1]) * (1.0 / (2 * half)) + 1e-06)
    squares[...] = jnp.broadcast_to(norm, (HD, tall_rows)).T

    def text_map(query, keys):
        scores = rows_by_rows(query, keys)
        weights = jnp.exp((scores - jnp.max(scores, axis=1, keepdims=True)) * scale)
        return weights * (1.0 / jnp.sum(weights, axis=1, keepdims=True))

    for chunk in range(chunks):
        for head in range(chunk * CHUNK, min(heads, (chunk + 1) * CHUNK)):
            at = slice(head * HD, (head + 1) * HD)
            gain = gains[:, pl.ds(pl.multiple_of(mine + head * HD, HD), HD)]
            middle = mid[:, :, at]
            query = middle.reshape(2 * rows, HD) * squares[0 : 2 * rows, :] * gain
            query = query.reshape(2, rows, HD).astype(jnp.bfloat16)
            source_map = text_map(query[0], text[0, :, at])
            edit_map = text_map(query[1], moved[0, :, at])
            injected = jnp.where(same > 0.5, source_map, edit_map)
            source_out = jnp.dot(
                source_map.astype(jnp.bfloat16),
                text[2, :, at],
                preferred_element_type=jnp.float32,
            )
            edit_out = jnp.dot(
                injected.astype(jnp.bfloat16),
                moved[1, :, at],
                preferred_element_type=jnp.float32,
            )
            out[0, :, at] = (middle[0] + source_out).astype(jnp.bfloat16)
            out[1, :, at] = (middle[1] + edit_out).astype(jnp.bfloat16)
        back_copy(1, chunk).start()
        own_out(1, chunk).start()

    for which in range(2):

        for piece in range((groups, chunks)[which]):
            back_copy(which, piece).wait()
            own_out(which, piece).wait()

        y_copy(which).wait_send()

    for which in range(classes):

        @pl.loop(0, tall)
        def _(lev):
            @pl.when(jnp.logical_not(relayed(lev, which)))
            def _():
                to_x(lev, which).wait_send()

            to_c(lev, 0, which).wait_send()
            to_c(lev, 1, which).wait_send()

            @pl.when(jnp.logical_and(has_above, lev <= level))
            def _():
                to_above(lev, which).wait_send()

            @pl.when(jnp.logical_and(has_below, lev >= level))
            def _():
                to_below(lev, which).wait_send()

        if which >= groups:

            @pl.when(relieved)
            def _():
                to_paired(which).wait_send()

    square_copy.wait_send()


def per_device(n, queries, keys_values, residual_in, cross_gain, text_kv, prompt_ids, word_align):
    rows, width = queries.shape[1:]
    half = keys_values.shape[2]
    heads = half // HD
    pairs = heads // PAIR
    text_len = word_align.shape[0]
    keys = n * rows
    tall = n // 4
    grouped = heads // 2 if heads % 2 == 0 else heads
    classes = 2 * heads // grouped
    tall_rows = pl.cdiv(2 * rows, HD) * HD
    vmem = pl.BlockSpec(memory_space=pltpu.VMEM)
    hbm = pl.BlockSpec(memory_space=pl.ANY)
    shape = jax.ShapeDtypeStruct((rows, width), jnp.bfloat16)
    bf16, f32 = jnp.bfloat16, jnp.float32
    dma = pltpu.SemaphoreType.DMA
    attended, result = pl.pallas_call(
        functools.partial(kernel, n),
        out_shape=(pltpu.VMEM((rows, width), bf16), pltpu.VMEM((rows, width), bf16)),
        in_specs=[hbm, hbm, hbm, vmem, hbm, vmem, vmem],
        out_specs=(vmem, vmem),
        scratch_shapes=[
            pltpu.VMEM((2, rows, half), bf16),
            pltpu.VMEM((2, rows, half), bf16),
            pltpu.VMEM((n, classes, rows, grouped * HD), bf16),
            pltpu.VMEM((4, text_len, half), bf16),
            pltpu.VMEM((2, text_len, half), bf16),
            pltpu.VMEM((text_len, text_len), bf16),
            pltpu.VMEM((heads, 2 * rows, keys), bf16),
            pltpu.VMEM((heads, 2 * rows, HD), f32),
            pltpu.VMEM((2, rows, half), bf16),
            pltpu.VMEM((2, rows, half), f32),
            pltpu.VMEM((tall_rows, HD), f32),
            pltpu.VMEM((2, 8, tall_rows), f32),
            pltpu.VMEM((1, width), f32),
            pltpu.VMEM((2, rows, half), bf16),
            dma((4,)),
            dma((2 + classes,)),
            dma((2, pairs)),
            dma((n, classes)),
            dma((tall, classes)),
            dma((tall, classes)),
            dma((tall, classes)),
            dma((2 * tall, classes)),
            dma((classes,)),
            dma((3,)),
            dma((3,)),
            dma((2, pairs)),
            dma((2, pairs)),
        ],
        compiler_params=pltpu.CompilerParams(
            collective_id=0, has_side_effects=True, vmem_limit_bytes=60 * 2**20
        ),
    )(
        queries[0],
        keys_values,
        residual_in[0],
        cross_gain,
        text_kv,
        prompt_ids,
        word_align[None],
    )
    return (attended[None], result[None])


def solution(mesh):
    in_specs = (
        P("branch", "seq", None),
        P(None, "seq", "branch"),
        P("branch", "seq", None),
        P(),
        P(),
        P(),
        P(),
    )
    out_specs = (P("branch", "seq", None), P("branch", "seq", None))
    return jax.shard_map(
        functools.partial(per_device, mesh.shape["seq"]),
        mesh=mesh,
        in_specs=in_specs,
        out_specs=out_specs,
        check_vma=False,
    )
```
